32 devices in a mesh: dp: 4 (over z), expert: 2 (over core), tensor: 4 (over y, x).
Axes of the slice: x: 2, y: 2, z: 4, core: 2. Of those that a mesh axis runs over, the one named last changes fastest.
Arguments:
- tokens: bfloat16 [4096, 6144], P(('dp', 'expert'), 'tensor'), parts along dimension 0, may hold values from -6 to 6
- route_ids: int32 [4096, 2], P(('dp', 'expert')), parts along dimension 0, may hold values from 0 to 7, as said below
- route_gates: float32 [4096, 2], P(('dp', 'expert')), parts along dimension 0, may hold values from 0.2 to 1
- w_gate: bfloat16 [2, 6144, 2048], P('expert', None, 'tensor'), may hold values from -0.078125 to 0.078125
- w_up: bfloat16 [2, 6144, 2048], P('expert', None, 'tensor'), may hold values from -0.078125 to 0.078125
- w_down: bfloat16 [2, 2048, 6144], P('expert', 'tensor'), may hold values from -0.125 to 0.125
Outputs:
- mixed: bfloat16 [4096, 6144], P(('dp', 'expert'), 'tensor'), parts along dimension 0
The draws below stay inside these ranges and needn't reach their ends.
There are 4 independent parts, one for each index of `dp`. The reference program is written for one: setup_inputs(seed, part) draws one part's arguments, and reference() takes and returns one part's arrays. A program takes and returns all parts, laid end to end along the dimension named above; an argument that names none is the same for every part. Nothing has to cross between parts.
Inputs may be any that keep to these rules, and one draw needn't show every extreme that they name: `route_ids`: in each aligned block of 512 rows (the rows of one expert index) every expert is named at most 256 times, and one expert below 2, the same in all blocks of a replica, is named exactly 256 times in every block. The 2 experts of a row differ.
All inputs are finite; a program needn't handle non-finite values.
Results may differ from the reference program's by a relative error of at most 0.0057.
Values may be sent and summed in bfloat16 or wider, within the bound.
A program may use at most 128 MiB of HBM per device.

```python
import jax
import jax.numpy as jnp
from jax import lax

D = 6144
ROUTED = 8
TOP = 2
TOK_DEV = 512
EXPERTS = 2
FF = 2048
TOKENS = 1024
CAP = 256


def shuffle_rows(key_one):
    return jax.random.permutation(key_one, TOK_DEV)


def draw_route_ids(key, part):
    key = jax.random.fold_in(key, 11)
    key_full, key_weights, key_order, key_swap = jax.random.split(key, 4)
    blocks = TOKENS // TOK_DEV
    others = ROUTED - 1
    remain = TOP * TOK_DEV - CAP
    full = jax.random.randint(key_full, (), 0, EXPERTS)
    weights = jax.random.randint(key_weights, (blocks, others), 2, 6)
    shares = remain * weights // jnp.sum(weights, axis=1, keepdims=True)
    shortfall = remain - jnp.sum(shares, axis=1, keepdims=True)
    shares = shares + (jnp.arange(others, dtype=jnp.int32)[None, :] < shortfall).astype(jnp.int32)
    expert_ids = jnp.arange(ROUTED, dtype=jnp.int32)
    other_index = expert_ids - (expert_ids > full).astype(jnp.int32)
    other_index = jnp.clip(other_index, 0, others - 1)
    counts = jnp.where(expert_ids[None, :] == full, CAP, jnp.take(shares, other_index, axis=1))
    ends = jnp.cumsum(counts, axis=1)
    slot_ids = jnp.arange(TOP * TOK_DEV, dtype=jnp.int32)
    labels = jnp.sum((ends[:, None, :] <= slot_ids[None, :, None]).astype(jnp.int32), axis=2)
    pairs = jnp.stack([labels[:, :TOK_DEV], labels[:, TOK_DEV:]], axis=2)
    orders = jax.vmap(shuffle_rows)(jax.random.split(key_order, blocks))
    pairs = jnp.take_along_axis(pairs, orders[:, :, None], axis=1)
    swapped = jax.random.randint(key_swap, (blocks, TOK_DEV, 1), 0, 2)
    pairs = jnp.where(swapped == 1, pairs[:, :, ::-1], pairs)
    return pairs.reshape(TOKENS, TOP).astype(jnp.int32)


def block_levels(key, shape, cuts, smallest, high):
    gain = 1.0
    for dim, parts in cuts:
        heights = jax.random.uniform(jax.random.fold_in(jax.random.fold_in(key, 6), dim), (parts,), jnp.float32, smallest / len(cuts), high / len(cuts))
        gain = gain * jnp.repeat(jnp.exp(heights), shape[dim] // parts).reshape((-1,) + (1,) * (len(shape) - 1 - dim))
    return gain


def gaussian(own_key, extent, scale, most, shards=(), kind=jnp.bfloat16):
    gain = block_levels(own_key, extent, shards, -0.22, 0.18) if shards else 1.0
    values = jax.random.normal(own_key, extent, jnp.float32) * scale * gain
    return jnp.minimum(jnp.maximum(values, -most), most).astype(kind)


def setup_inputs(seed: int = 0, part: int = 0) -> dict:
    key_list = jax.random.split(jax.random.key(seed), 7)
    part_keys = jax.random.split(jax.random.fold_in(key_list[6], part), 7)
    return {
        "tokens": gaussian(part_keys[0], (TOKENS, D), 1.0, 6.0, ((0, 2), (1, 4))),
        "route_ids": draw_route_ids(jax.random.fold_in(jax.random.fold_in(key_list[6], part), 71), part),
        "route_gates": jnp.clip(0.2 + 0.8 * jax.random.uniform(part_keys[2], (TOKENS, TOP), jnp.float32) ** block_levels(part_keys[2], (TOKENS, TOP), ((0, 2),), -0.2, 0.2), 0.2, 1.0),
        "w_gate": gaussian(key_list[3], (EXPERTS, D, FF), D ** -0.5, 0.078125, ((0, 2), (2, 4))),
        "w_up": gaussian(key_list[4], (EXPERTS, D, FF), D ** -0.5, 0.078125, ((0, 2), (2, 4))),
        "w_down": gaussian(key_list[5], (EXPERTS, FF, D), FF ** -0.5, 0.125, ((0, 2), (1, 4))),
    }


def reference(tokens, route_ids, route_gates, w_gate, w_up, w_down):
    def one_expert(total, index):
        weight = jnp.sum(jnp.where(route_ids == index, route_gates, 0.0), axis=1)
        gate = jnp.dot(tokens, w_gate[index], preferred_element_type=jnp.float32)
        upper = jnp.dot(tokens, w_up[index], preferred_element_type=jnp.float32)
        gated = (jax.nn.silu(gate) * upper).astype(jnp.bfloat16)
        result = jnp.dot(gated, w_down[index], preferred_element_type=jnp.float32).astype(jnp.bfloat16)
        return total + weight[:, None] * result.astype(jnp.float32), None

    start = jnp.zeros(tokens.shape, jnp.float32)
    total, unused = lax.scan(one_expert, start, jnp.arange(EXPERTS, dtype=jnp.int32))
    return total.astype(jnp.bfloat16)
```

```python
import functools

import jax
import jax.numpy as jnp
from jax import lax
from jax.experimental import pallas as pl
from jax.experimental.pallas import tpu as pltpu
from jax.sharding import PartitionSpec as P

MESH = pl.DeviceIdType.MESH
AG1X, AG1Y, AG2X, AG2Y, RS1X, RS1Y, RS2X, RS2Y, RET = range(9)


def moe_kernel(
    rows_full,
    chunk,
    ahead,
    tok_ref,
    idr_ref,
    idc_ref,
    gat_ref,
    wg_hbm,
    wu_hbm,
    wd_hbm,
    out_ref,
    xg,
    wg,
    wu,
    wd,
    dsp,
    snd_d,
    snd_x,
    snd_y,
    got_d,
    got_x,
    got_y,
    own,
    back,
    ret,
    pt_own,
    pt_oth,
    send_sem,
    recv_sem,
    wsem,
    dsem,
):
    cap = rows_full
    tok_rows, width = tok_ref.shape
    nch = 2 * cap // chunk
    half_ch = nch // 2
    hc = chunk // 2
    e = lax.axis_index("expert")
    t = lax.axis_index("tensor")
    tx = (t // 2) * 2 + (1 - t % 2)
    ty = (1 - t // 2) * 2 + t % 2
    td = 3 - t

    barrier = pltpu.get_barrier_semaphore()
    pl.semaphore_signal(barrier, inc=1, device_id={"expert": 1 - e}, device_id_type=MESH)
    pl.semaphore_signal(barrier, inc=1, device_id={"tensor": tx}, device_id_type=MESH)
    pl.semaphore_signal(barrier, inc=1, device_id={"tensor": ty}, device_id_type=MESH)

    def weight_copies():
        copies = [
            pltpu.make_async_copy(wg_hbm, wg, wsem.at[0]),
            pltpu.make_async_copy(wu_hbm, wu, wsem.at[1]),
        ]
        for s in range(4):
            copies.append(
                pltpu.make_async_copy(
                    wd_hbm.at[:, pl.ds(s * width, width)], wd.at[s], wsem.at[2 + s]
                )
            )
        return copies

    for c in weight_copies():
        c.start()

    def rows(k):
        return pl.ds(pl.multiple_of(k * chunk, chunk), chunk)

    def first(k):
        return pl.ds(pl.multiple_of(k * chunk, hc), hc)

    def second(k):
        return pl.ds(pl.multiple_of(k * chunk + hc, hc), hc)

    def remote(kind, k, src, dst, device):
        return pltpu.make_async_remote_copy(
            src_ref=src,
            dst_ref=dst,
            send_sem=send_sem.at[kind, k],
            recv_sem=recv_sem.at[kind, k],
            device_id=device,
            device_id_type=MESH,
        )

    to_x, to_y, to_p = {"tensor": tx}, {"tensor": ty}, {"expert": 1 - e}

    def ag1x(k):
        return remote(AG1X, k, xg.at[t, rows(k)], xg.at[t, rows(k)], to_x)

    def ag1y(k):
        return remote(AG1Y, k, xg.at[t, rows(k)], xg.at[t, rows(k)], to_y)

    def ag2x(k):
        return remote(AG2X, k, xg.at[ty, second(k)], xg.at[ty, second(k)], to_x)

    def ag2y(k):
        return remote(AG2Y, k, xg.at[tx, first(k)], xg.at[tx, first(k)], to_y)

    def rs1x(k):
        return remote(RS1X, k, snd_d.at[first(k)], got_d.at[first(k)], to_x)

    def rs1y(k):
        return remote(RS1Y, k, snd_d.at[second(k)], got_d.at[second(k)], to_y)

    def rs2x(k):
        return remote(RS2X, k, snd_x.at[rows(k)], got_x.at[rows(k)], to_x)

    def rs2y(k):
        return remote(RS2Y, k, snd_y.at[rows(k)], got_y.at[rows(k)], to_y)

    def give(k):
        return remote(RET, k, ret.at[rows(k)], back.at[1, rows(k)], to_p)

    dispatch = pltpu.make_async_remote_copy(
        src_ref=dsp,
        dst_ref=xg.at[t, pl.ds(cap, cap)],
        send_sem=dsem.at[0],
        recv_sem=dsem.at[1],
        device_id=to_p,
        device_id_type=MESH,
    )

    before = (
        lax.broadcasted_iota(jnp.int32, (tok_rows, tok_rows), 0)
        < lax.broadcasted_iota(jnp.int32, (tok_rows, tok_rows), 1)
    )
    before = jnp.where(before, 1.0, 0.0).astype(jnp.bfloat16)

    def onehot(expert):
        named = (idr_ref[0:1, :] == expert) | (idr_ref[1:2, :] == expert)
        named = jnp.where(named, 1.0, 0.0)
        wide = jnp.broadcast_to(named, (16, tok_rows)).astype(jnp.bfloat16)
        pos = jnp.dot(wide, before, preferred_element_type=jnp.float32)[0:1, :]
        pos = jnp.where(named > 0.5, pos, -1.0).astype(jnp.int32)
        slot = lax.broadcasted_iota(jnp.int32, (cap, tok_rows), 0)
        return jnp.where(slot == pos, 1.0, 0.0)

    tok = tok_ref[...]
    pick_own = onehot(e)
    xg[t, 0:cap] = jnp.dot(
        pick_own.astype(jnp.bfloat16), tok, preferred_element_type=jnp.float32
    ).astype(jnp.bfloat16)
    pl.semaphore_wait(barrier, 3)
    for k in range(min(ahead, half_ch)):
        ag1x(k).start()
        ag1y(k).start()
    pick_oth = onehot(1 - e)
    dsp[...] = jnp.dot(
        pick_oth.astype(jnp.bfloat16), tok, preferred_element_type=jnp.float32
    ).astype(jnp.bfloat16)
    dispatch.start()
    pt_own[...] = pick_own.T.astype(jnp.bfloat16)
    pt_oth[...] = pick_oth.T.astype(jnp.bfloat16)

    def step(i, carry):
        @pl.when(i + ahead == half_ch)
        def _():
            dispatch.wait_recv()

        @pl.when(i + ahead < nch)
        def _():
            ag1x(i + ahead).start()
            ag1y(i + ahead).start()

        @pl.when(i < nch)
        def _():
            ag1x(i).wait_recv()
            ag2y(i).start()
            ag1y(i).wait_recv()
            ag2x(i).start()

        @pl.when(i == 1)
        def _():
            for c in weight_copies():
                c.wait()

        @pl.when((i >= 1) & (i - 1 < nch))
        def _():
            k = i - 1
            ag2x(k).wait_recv()
            ag2y(k).wait_recv()
            gate = jnp.zeros((chunk, wg.shape[2]), jnp.float32)
            upper = gate
            for s in range(4):
                part = xg[s, rows(k), :]
                gate += jnp.dot(part, wg[s], preferred_element_type=jnp.float32)
                upper += jnp.dot(part, wu[s], preferred_element_type=jnp.float32)
            gated = (gate / (1.0 + jnp.exp(-gate)) * upper).astype(jnp.bfloat16)
            snd_d[rows(k), :] = jnp.dot(
                gated, wd[td], preferred_element_type=jnp.float32
            ).astype(jnp.bfloat16)
            rs1x(k).start()
            rs1y(k).start()
            snd_x[rows(k), :] = jnp.dot(
                gated, wd[tx], preferred_element_type=jnp.float32
            ).astype(jnp.bfloat16)
            snd_y[rows(k), :] = jnp.dot(
                gated, wd[ty], preferred_element_type=jnp.float32
            ).astype(jnp.bfloat16)
            own[rows(k), :] = jnp.dot(gated, wd[t], preferred_element_type=jnp.float32)

        @pl.when((i >= 2) & (i - 2 < nch))
        def _():
            k = i - 2
            rs1x(k).wait_recv()
            snd_y[first(k), :] = (
                snd_y[first(k), :].astype(jnp.float32) + got_d[first(k), :].astype(jnp.float32)
            ).astype(jnp.bfloat16)
            rs2y(k).start()
            rs1y(k).wait_recv()
            snd_x[second(k), :] = (
                snd_x[second(k), :].astype(jnp.float32) + got_d[second(k), :].astype(jnp.float32)
            ).astype(jnp.bfloat16)
            rs2x(k).start()

        @pl.when(i >= 3)
        def _():
            k = i - 3
            rs2x(k).wait_recv()
            rs2y(k).wait_recv()
            done = (
                own[rows(k), :]
                + got_x[rows(k), :].astype(jnp.float32)
                + got_y[rows(k), :].astype(jnp.float32)
            ).astype(jnp.bfloat16)

            @pl.when(k < half_ch)
            def _():
                back[0, rows(k), :] = done

            @pl.when(k >= half_ch)
            def _():
                ret[rows(k - half_ch), :] = done
                give(k - half_ch).start()

        return carry

    lax.fori_loop(0, nch + 3, step, 0)

    def weight_of(expert):
        ids = idc_ref[...]
        gates = gat_ref[...]
        return jnp.sum(jnp.where(ids == expert, gates, 0.0), axis=1, keepdims=True)

    mine = weight_of(e) * jnp.dot(pt_own[...], back[0], preferred_element_type=jnp.float32)

    def landed(k, carry):
        give(k).wait_recv()
        return carry

    lax.fori_loop(0, half_ch, landed, 0)
    theirs = weight_of(1 - e) * jnp.dot(pt_oth[...], back[1], preferred_element_type=jnp.float32)
    out_ref[...] = (mine + theirs).astype(jnp.bfloat16)

    dispatch.wait_send()

    def drain(k, carry):
        for make in (ag1x, ag1y, ag2x, ag2y, rs1x, rs1y, rs2x, rs2y):
            make(k).wait_send()
        return carry

    lax.fori_loop(0, nch, drain, 0)

    def drain_give(k, carry):
        give(k).wait_send()
        return carry

    lax.fori_loop(0, half_ch, drain_give, 0)


def fused(tokens, route_ids, route_gates, w_gate, w_up, w_down):
    tok_rows, width = tokens.shape
    tensor = lax.axis_size("tensor")
    cap = tok_rows // 2
    chunk = 128
    ahead = 2
    hidden = w_gate.shape[2]
    total = 2 * cap
    nch = total // chunk
    bf16 = jnp.bfloat16
    vmem = pl.BlockSpec(memory_space=pltpu.VMEM)
    hbm = pl.BlockSpec(memory_space=pl.ANY)
    flops = 2 * total * tensor * width * hidden * 3
    return pl.pallas_call(
        functools.partial(moe_kernel, cap, chunk, ahead),
        out_shape=jax.ShapeDtypeStruct((tok_rows, width), bf16),
        in_specs=[vmem, vmem, vmem, vmem, hbm, hbm, hbm],
        out_specs=vmem,
        scratch_shapes=[
            pltpu.VMEM((tensor, total, width), bf16),
            pltpu.VMEM((tensor, width, hidden), bf16),
            pltpu.VMEM((tensor, width, hidden), bf16),
            pltpu.VMEM((tensor, hidden, width), bf16),
            pltpu.VMEM((cap, width), bf16),
            pltpu.VMEM((total, width), bf16),
            pltpu.VMEM((total, width), bf16),
            pltpu.VMEM((total, width), bf16),
            pltpu.VMEM((total, width), bf16),
            pltpu.VMEM((total, width), bf16),
            pltpu.VMEM((total, width), bf16),
            pltpu.VMEM((total, width), jnp.float32),
            pltpu.VMEM((2, cap, width), bf16),
            pltpu.VMEM((cap, width), bf16),
            pltpu.VMEM((tok_rows, cap), bf16),
            pltpu.VMEM((tok_rows, cap), bf16),
            pltpu.SemaphoreType.DMA((9, nch)),
            pltpu.SemaphoreType.DMA((9, nch)),
            pltpu.SemaphoreType.DMA((6,)),
            pltpu.SemaphoreType.DMA((2,)),
        ],
        compiler_params=pltpu.CompilerParams(
            collective_id=0, has_side_effects=True, vmem_limit_bytes=60 * 1024 * 1024
        ),
        cost_estimate=pl.CostEstimate(
            flops=flops, bytes_accessed=3 * tensor * width * hidden * 2, transcendentals=0
        ),
    )(
        tokens,
        route_ids.T,
        route_ids,
        route_gates,
        w_gate.reshape(tensor, width, hidden),
        w_up.reshape(tensor, width, hidden),
        w_down.reshape(hidden, tensor * width),
    )


def general(tokens, route_ids, route_gates, w_gate, w_up, w_down):
    tok_rows, width_dev = tokens.shape
    picks = route_ids.shape[1]
    n_source = lax.axis_size("expert")
    local_count = w_gate.shape[0]
    n_flight = n_source * local_count
    capacity = tok_rows // 2
    flat_ids = route_ids.reshape(-1)
    onehot = (flat_ids[:, None] == jnp.arange(n_flight, dtype=jnp.int32)[None, :]).astype(jnp.int32)
    earlier = jnp.cumsum(onehot, axis=0) - onehot
    position = jnp.sum(earlier * onehot, axis=1)
    in_window = flat_ids < n_flight
    slots = jnp.where(in_window, flat_ids * capacity + position, n_flight * capacity)
    repeated = jnp.repeat(tokens, picks, axis=0)
    buffer = (
        jnp.zeros((n_flight * capacity, width_dev), jnp.bfloat16)
        .at[slots]
        .set(repeated, mode="drop")
    )
    buffer = buffer.reshape(n_flight, capacity, width_dev)
    received = lax.all_to_all(buffer, "expert", split_axis=0, concat_axis=0, tiled=True)
    piece = lax.all_gather(received, "tensor", axis=2, tiled=True)
    columns = piece.shape[2]
    grouped = piece.reshape(n_source, local_count, capacity, columns)
    gate = jnp.einsum("secd,edf->secf", grouped, w_gate, preferred_element_type=jnp.float32)
    upper = jnp.einsum("secd,edf->secf", grouped, w_up, preferred_element_type=jnp.float32)
    gated = (jax.nn.silu(gate) * upper).astype(jnp.bfloat16)
    partial_out = jnp.einsum("secf,efd->secd", gated, w_down, preferred_element_type=jnp.float32)
    partial_out = partial_out.reshape(n_flight, capacity, partial_out.shape[3])
    summed = lax.psum_scatter(partial_out, "tensor", scatter_dimension=2, tiled=True)
    expert_out = summed.astype(jnp.bfloat16)
    back = lax.all_to_all(expert_out, "expert", split_axis=0, concat_axis=0, tiled=True)
    flat_back = back.reshape(n_flight * capacity, width_dev)
    picked = jnp.take(flat_back, slots, axis=0, mode="fill", fill_value=0).astype(jnp.float32)
    picked = picked.reshape(tok_rows, picks, width_dev)
    mixed = jnp.sum(picked * route_gates[:, :, None], axis=1)
    return mixed.astype(jnp.bfloat16)


def solution(mesh):
    placed = (
        P(("dp", "expert"), "tensor"),
        P(("dp", "expert"), None),
        P(("dp", "expert"), None),
        P("expert", None, "tensor"),
        P("expert", None, "tensor"),
        P("expert", "tensor", None),
    )
    square = mesh.shape["tensor"] == 4 and mesh.shape["expert"] == 2
    return jax.shard_map(
        fused if square else general,
        mesh=mesh,
        in_specs=placed,
        out_specs=P(("dp", "expert"), "tensor"),
        check_vma=False,
    )
```

```python
import functools

import jax
import jax.numpy as jnp
from jax import lax
from jax.experimental import pallas as pl
from jax.experimental.pallas import tpu as pltpu
from jax.sharding import PartitionSpec as P

MESH = pl.DeviceIdType.MESH
AG1X, AG1Y, AG2X, AG2Y, RS1X, RS1Y, RS2X, RS2Y, RET = range(9)


def moe_kernel(
    plan,
    tok_ref,
    ids_ref,
    gat_ref,
    off_ref,
    wg_hbm,
    wu_hbm,
    wd_hbm,
    out_ref,
    xg,
    wg,
    wu,
    wd,
    dsp,
    mrg,
    snd_d,
    snd_x,
    snd_y,
    got_d,
    got_x,
    got_y,
    own,
    back,
    ret,
    pt_own,
    pt_oth,
    send_sem,
    recv_sem,
    wsem,
    dsem,
):
    tok_rows, width = tok_ref.shape
    e = lax.axis_index("expert")
    t = lax.axis_index("tensor")
    tx = (t // 2) * 2 + (1 - t % 2)
    ty = (1 - t // 2) * 2 + t % 2
    td = 3 - t
    to_x, to_y, to_p = {"tensor": tx}, {"tensor": ty}, {"expert": 1 - e}

    barrier = pltpu.get_barrier_semaphore()
    for device in (to_p, to_x, to_y):
        pl.semaphore_signal(barrier, inc=1, device_id=device, device_id_type=MESH)

    def weight_copies():
        copies = [
            pltpu.make_async_copy(wg_hbm, wg, wsem.at[0]),
            pltpu.make_async_copy(wu_hbm, wu, wsem.at[1]),
        ]
        for s in range(4):
            copies.append(
                pltpu.make_async_copy(
                    wd_hbm.at[:, pl.ds(s * width, width)], wd.at[s], wsem.at[2 + s]
                )
            )
        return copies

    for c in weight_copies():
        c.start()

    before = (
        lax.broadcasted_iota(jnp.int32, (tok_rows, tok_rows), 0)
        < lax.broadcasted_iota(jnp.int32, (tok_rows, tok_rows), 1)
    )
    before = jnp.where(before, 1.0, 0.0).astype(jnp.bfloat16)

    def onehot(expert, count, offset):
        named = (ids_ref[0:1, :] == expert) | (ids_ref[1:2, :] == expert)
        named = jnp.where(named, 1.0, 0.0)
        wide = jnp.broadcast_to(named, (16, tok_rows)).astype(jnp.bfloat16)
        pos = jnp.dot(wide, before, preferred_element_type=jnp.float32)[0:1, :]
        pos = jnp.where(named > 0.5, pos, -2.0 * tok_rows).astype(jnp.int32) + offset
        slot = lax.broadcasted_iota(jnp.int32, (count, tok_rows), 0)
        return jnp.where(slot == pos, 1.0, 0.0)

    def gate_column(expert):
        row = jnp.where(ids_ref[0:1, :] == expert, gat_ref[0:1, :], 0.0)
        row += jnp.where(ids_ref[1:2, :] == expert, gat_ref[1:2, :], 0.0)
        return jnp.broadcast_to(row, (8, tok_rows)).T[:, 0:1]

    def body(me):
        total, chunk, packed = plan[me]
        oth_total, oth_chunk, oth_packed = plan[1 - me]
        nch = total // chunk
        hc = chunk // 2
        lead = total if packed else total // 2
        give_rows = oth_total if oth_packed else oth_total // 2
        take_rows = total if packed else total // 2
        ahead = 2
        ret_from = 0 if packed else nch // 2
        oth_back = oth_total // oth_chunk if oth_packed else oth_total // oth_chunk // 2

        def rows(k):
            return pl.ds(pl.multiple_of(k * chunk, hc), chunk)

        def first(k):
            return pl.ds(pl.multiple_of(k * chunk, hc), hc)

        def second(k):
            return pl.ds(pl.multiple_of(k * chunk + hc, hc), hc)

        def remote(kind, k, src, dst, device):
            return pltpu.make_async_remote_copy(
                src_ref=src,
                dst_ref=dst,
                send_sem=send_sem.at[kind, k],
                recv_sem=recv_sem.at[kind, k],
                device_id=device,
                device_id_type=MESH,
            )

        def ag1x(k):
            return remote(AG1X, k, xg.at[t, rows(k)], xg.at[t, rows(k)], to_x)

        def ag1y(k):
            return remote(AG1Y, k, xg.at[t, rows(k)], xg.at[t, rows(k)], to_y)

        def ag2x(k):
            return remote(AG2X, k, xg.at[ty, second(k)], xg.at[ty, second(k)], to_x)

        def ag2y(k):
            return remote(AG2Y, k, xg.at[tx, first(k)], xg.at[tx, first(k)], to_y)

        def rs1x(k):
            return remote(RS1X, k, snd_d.at[first(k)], got_d.at[first(k)], to_x)

        def rs1y(k):
            return remote(RS1Y, k, snd_d.at[second(k)], got_d.at[second(k)], to_y)

        def rs2x(k):
            return remote(RS2X, k, snd_x.at[rows(k)], got_x.at[rows(k)], to_x)

        def rs2y(k):
            return remote(RS2Y, k, snd_y.at[rows(k)], got_y.at[rows(k)], to_y)

        def give(k):
            return remote(RET, k, ret.at[rows(k)], back.at[1, rows(k)], to_p)

        def take(k):
            there = pl.ds(pl.multiple_of(k * oth_chunk, oth_chunk // 2), oth_chunk)
            return remote(RET, k, ret.at[there], back.at[1, there], to_p)

        def hand(count):
            return pltpu.make_async_remote_copy(
                src_ref=dsp.at[pl.ds(0, count)],
                dst_ref=mrg.at[pl.ds(0, count)],
                send_sem=dsem.at[0],
                recv_sem=dsem.at[1],
                device_id=to_p,
                device_id_type=MESH,
            )

        tok = tok_ref[...]

        def own_rows():
            pick = onehot(me, lead, 0)
            mine = jnp.dot(pick.astype(jnp.bfloat16), tok, preferred_element_type=jnp.float32)
            xg[t, 0:lead] = mine.astype(jnp.bfloat16)
            pt_own[:, 0:lead] = pick.T.astype(jnp.bfloat16)

        def other_rows():
            pick = onehot(1 - me, give_rows, off_ref[0:1, 0:1] if oth_packed else 0)
            theirs = jnp.dot(pick.astype(jnp.bfloat16), tok, preferred_element_type=jnp.float32)
            dsp[0:give_rows, :] = theirs.astype(jnp.bfloat16)
            pt_oth[:, 0:give_rows] = pick.T.astype(jnp.bfloat16)

        def ready(k):
            ag1x(k).start()
            ag1y(k).start()

        if packed:
            other_rows()
            pl.semaphore_wait(barrier, 3)
            hand(give_rows).start()
            own_rows()
            hand(take_rows).wait_recv()
            xg[t, 0:total] = xg[t, 0:total] + mrg[0:total, :]
            for k in range(min(ahead, nch)):
                ready(k)
        else:
            own_rows()
            pl.semaphore_wait(barrier, 3)
            for k in range(min(ahead, nch // 2)):
                ready(k)
            other_rows()
            hand(give_rows).start()

        def step(i, carry):
            if not packed:

                @pl.when(i + ahead == nch // 2)
                def _():
                    hand(take_rows).wait_recv()
                    xg[t, lead:total] = mrg[0:take_rows, :]

            @pl.when(i + ahead < nch)
            def _():
                ready(i + ahead)

            @pl.when(i < nch)
            def _():
                ag1x(i).wait_recv()
                ag2y(i).start()
                ag1y(i).wait_recv()
                ag2x(i).start()

            @pl.when(i == 1)
            def _():
                for c in weight_copies():
                    c.wait()

            @pl.when((i >= 1) & (i - 1 < nch))
            def _():
                k = i - 1
                ag2x(k).wait_recv()
                ag2y(k).wait_recv()
                gate = jnp.zeros((chunk, wg.shape[2]), jnp.float32)
                upper = gate
                for s in range(4):
                    part = xg[s, rows(k), :]
                    gate += jnp.dot(part, wg[s], preferred_element_type=jnp.float32)
                    upper += jnp.dot(part, wu[s], preferred_element_type=jnp.float32)
                gated = (gate / (1.0 + jnp.exp(-gate)) * upper).astype(jnp.bfloat16)
                snd_d[rows(k), :] = jnp.dot(
                    gated, wd[td], preferred_element_type=jnp.float32
                ).astype(jnp.bfloat16)
                rs1x(k).start()
                rs1y(k).start()
                snd_x[rows(k), :] = jnp.dot(
                    gated, wd[tx], preferred_element_type=jnp.float32
                ).astype(jnp.bfloat16)
                snd_y[rows(k), :] = jnp.dot(
                    gated, wd[ty], preferred_element_type=jnp.float32
                ).astype(jnp.bfloat16)
                own[rows(k), :] = jnp.dot(gated, wd[t], preferred_element_type=jnp.float32)

            @pl.when((i >= 2) & (i - 2 < nch))
            def _():
                k = i - 2
                rs1x(k).wait_recv()
                snd_y[first(k), :] = (
                    snd_y[first(k), :].astype(jnp.float32)
                    + got_d[first(k), :].astype(jnp.float32)
                ).astype(jnp.bfloat16)
                rs2y(k).start()
                rs1y(k).wait_recv()
                snd_x[second(k), :] = (
                    snd_x[second(k), :].astype(jnp.float32)
                    + got_d[second(k), :].astype(jnp.float32)
                ).astype(jnp.bfloat16)
                rs2x(k).start()

            @pl.when(i >= 3)
            def _():
                k = i - 3
                rs2x(k).wait_recv()
                rs2y(k).wait_recv()
                done = (
                    own[rows(k), :]
                    + got_x[rows(k), :].astype(jnp.float32)
                    + got_y[rows(k), :].astype(jnp.float32)
                ).astype(jnp.bfloat16)
                if packed:
                    back[0, rows(k), :] = done
                    ret[rows(k), :] = done
                    give(k).start()
                else:

                    @pl.when(k < ret_from)
                    def _():
                        back[0, rows(k), :] = done

                    @pl.when(k >= ret_from)
                    def _():
                        ret[rows(k - ret_from), :] = done
                        give(k - ret_from).start()

            return carry

        lax.fori_loop(0, nch + 3, step, 0)

        mine = gate_column(me) * jnp.dot(
            pt_own[:, 0:lead], back[0, 0:lead, :], preferred_element_type=jnp.float32
        )

        def landed(k, carry):
            take(k).wait_recv()
            return carry

        lax.fori_loop(0, oth_back, landed, 0)
        theirs = gate_column(1 - me) * jnp.dot(
            pt_oth[:, 0:give_rows], back[1, 0:give_rows, :], preferred_element_type=jnp.float32
        )
        out_ref[...] = (mine + theirs).astype(jnp.bfloat16)

        hand(give_rows).wait_send()

        def drain(k, carry):
            for make in (ag1x, ag1y, ag2x, ag2y, rs1x, rs1y, rs2x, rs2y):
                make(k).wait_send()
            return carry

        lax.fori_loop(0, nch, drain, 0)

        def drain_give(k, carry):
            give(k).wait_send()
            return carry

        lax.fori_loop(0, nch - ret_from, drain_give, 0)

    for core in range(2):
        pl.when(e == core)(functools.partial(body, core))


def moe_call(plan, number, tokens, ids, gates, offset, w_gate, w_up, w_down):
    tok_rows, width = tokens.shape
    tensor, _, hidden = w_gate.shape
    total = max(p[0] for p in plan)
    lead = max(p[0] if p[2] else p[0] // 2 for p in plan)
    nch = max(p[0] // p[1] for p in plan)
    bf16 = jnp.bfloat16
    vmem = pl.BlockSpec(memory_space=pltpu.VMEM)
    hbm = pl.BlockSpec(memory_space=pl.ANY)
    return pl.pallas_call(
        functools.partial(moe_kernel, plan),
        out_shape=jax.ShapeDtypeStruct((tok_rows, width), bf16),
        in_specs=[vmem, vmem, vmem, vmem, hbm, hbm, hbm],
        out_specs=vmem,
        scratch_shapes=[
            pltpu.VMEM((tensor, total, width), bf16),
            pltpu.VMEM((tensor, width, hidden), bf16),
            pltpu.VMEM((tensor, width, hidden), bf16),
            pltpu.VMEM((tensor, hidden, width), bf16),
            pltpu.VMEM((lead, width), bf16),
            pltpu.VMEM((lead, width), bf16),
            pltpu.VMEM((total, width), bf16),
            pltpu.VMEM((total, width), bf16),
            pltpu.VMEM((total, width), bf16),
            pltpu.VMEM((total, width), bf16),
            pltpu.VMEM((total, width), bf16),
            pltpu.VMEM((total, width), bf16),
            pltpu.VMEM((total, width), jnp.float32),
            pltpu.VMEM((2, lead, width), bf16),
            pltpu.VMEM((lead, width), bf16),
            pltpu.VMEM((tok_rows, lead), bf16),
            pltpu.VMEM((tok_rows, lead), bf16),
            pltpu.SemaphoreType.DMA((9, nch)),
            pltpu.SemaphoreType.DMA((9, nch)),
            pltpu.SemaphoreType.DMA((6,)),
            pltpu.SemaphoreType.DMA((2,)),
        ],
        compiler_params=pltpu.CompilerParams(
            collective_id=number, has_side_effects=True, vmem_limit_bytes=60 * 1024 * 1024
        ),
        cost_estimate=pl.CostEstimate(
            flops=6 * total * tensor * width * hidden,
            bytes_accessed=6 * tensor * width * hidden,
            transcendentals=0,
        ),
    )(tokens, ids, gates, offset, w_gate, w_up, w_down)


def fused(tokens, route_ids, route_gates, w_gate, w_up, w_down):
    tok_rows, width = tokens.shape
    tensor = lax.axis_size("tensor")
    hidden = w_gate.shape[2]
    e = lax.axis_index("expert")
    ids, gates = route_ids.T, route_gates.T
    counts = jnp.sum(
        (ids[:, :, None] == jnp.arange(2, dtype=jnp.int32)).astype(jnp.int32), axis=(0, 1)
    )
    theirs = lax.ppermute(counts, "expert", [(0, 1), (1, 0)])
    totals = counts + theirs
    offset = jnp.broadcast_to(theirs[1 - e], (8, 128))
    full = tok_rows
    whole = (full, full // 4, False)
    sizes = ((full // 2, full // 4), (full * 9 // 16, full * 3 // 16), (full * 5 // 8, full * 5 // 16))
    plans = []
    for packed_rows, packed_chunk in sizes:
        small = (packed_rows, packed_chunk, True)
        plans += [(whole, small), (small, whole)]
    plans.append((whole, whole))
    least = jnp.min(totals)
    level = sum((least > s).astype(jnp.int32) for s, _ in sizes)
    heavy = (totals[1] > totals[0]).astype(jnp.int32)
    index = jnp.minimum(2 * level + heavy, 2 * len(sizes))
    branches = [functools.partial(moe_call, plan, n) for n, plan in enumerate(plans)]
    return lax.switch(
        index,
        branches,
        tokens,
        ids,
        gates,
        offset,
        w_gate.reshape(tensor, width, hidden),
        w_up.reshape(tensor, width, hidden),
        w_down.reshape(hidden, tensor * width),
    )


def general(tokens, route_ids, route_gates, w_gate, w_up, w_down):
    tok_rows, width_dev = tokens.shape
    picks = route_ids.shape[1]
    n_source = lax.axis_size("expert")
    local_count = w_gate.shape[0]
    n_flight = n_source * local_count
    capacity = tok_rows // 2
    flat_ids = route_ids.reshape(-1)
    onehot = (flat_ids[:, None] == jnp.arange(n_flight, dtype=jnp.int32)[None, :]).astype(jnp.int32)
    earlier = jnp.cumsum(onehot, axis=0) - onehot
    position = jnp.sum(earlier * onehot, axis=1)
    in_window = flat_ids < n_flight
    slots = jnp.where(in_window, flat_ids * capacity + position, n_flight * capacity)
    repeated = jnp.repeat(tokens, picks, axis=0)
    buffer = (
        jnp.zeros((n_flight * capacity, width_dev), jnp.bfloat16)
        .at[slots]
        .set(repeated, mode="drop")
    )
    buffer = buffer.reshape(n_flight, capacity, width_dev)
    received = lax.all_to_all(buffer, "expert", split_axis=0, concat_axis=0, tiled=True)
    piece = lax.all_gather(received, "tensor", axis=2, tiled=True)
    columns = piece.shape[2]
    grouped = piece.reshape(n_source, local_count, capacity, columns)
    gate = jnp.einsum("secd,edf->secf", grouped, w_gate, preferred_element_type=jnp.float32)
    upper = jnp.einsum("secd,edf->secf", grouped, w_up, preferred_element_type=jnp.float32)
    gated = (jax.nn.silu(gate) * upper).astype(jnp.bfloat16)
    partial_out = jnp.einsum("secf,efd->secd", gated, w_down, preferred_element_type=jnp.float32)
    partial_out = partial_out.reshape(n_flight, capacity, partial_out.shape[3])
    summed = lax.psum_scatter(partial_out, "tensor", scatter_dimension=2, tiled=True)
    expert_out = summed.astype(jnp.bfloat16)
    back = lax.all_to_all(expert_out, "expert", split_axis=0, concat_axis=0, tiled=True)
    flat_back = back.reshape(n_flight * capacity, width_dev)
    picked = jnp.take(flat_back, slots, axis=0, mode="fill", fill_value=0).astype(jnp.float32)
    picked = picked.reshape(tok_rows, picks, width_dev)
    mixed = jnp.sum(picked * route_gates[:, :, None], axis=1)
    return mixed.astype(jnp.bfloat16)


def solution(mesh):
    placed = (
        P(("dp", "expert"), "tensor"),
        P(("dp", "expert"), None),
        P(("dp", "expert"), None),
        P("expert", None, "tensor"),
        P("expert", None, "tensor"),
        P("expert", "tensor", None),
    )
    square = mesh.shape["tensor"] == 4 and mesh.shape["expert"] == 2
    return jax.shard_map(
        fused if square else general,
        mesh=mesh,
        in_specs=placed,
        out_specs=P(("dp", "expert"), "tensor"),
        check_vma=False,
    )
```

```python
import functools

import jax
import jax.numpy as jnp
from jax import lax
from jax.experimental import pallas as pl
from jax.experimental.pallas import tpu as pltpu
from jax.sharding import PartitionSpec as P

MESH = pl.DeviceIdType.MESH
AG1X, AG1Y, AG2X, AG2Y, RS1X, RS1Y, RS2X, RS2Y, RET, HAND = range(10)


def moe_kernel(
    heavy_core,
    light_rows,
    chunk,
    ahead,
    tok_ref,
    ids_ref,
    gat_ref,
    off_ref,
    wg_hbm,
    wu_hbm,
    wd_hbm,
    out_ref,
    xg,
    wgu,
    wd,
    dsp,
    mrg,
    acc,
    snd,
    got_d,
    got_x,
    got_y,
    own,
    back,
    pt_own,
    pt_oth,
    send_sem,
    recv_sem,
    wsem,
):
    tok_rows, width = tok_ref.shape
    hidden = wgu.shape[3]
    cap = tok_rows // 2
    hc = chunk // 2
    tile = width // 3
    e = lax.axis_index("expert")
    t = lax.axis_index("tensor")
    tx = (t // 2) * 2 + (1 - t % 2)
    ty = (1 - t // 2) * 2 + t % 2
    td = 3 - t
    to_x, to_y, to_p = {"tensor": tx}, {"tensor": ty}, {"expert": 1 - e}
    most, least = tok_rows // chunk, light_rows // chunk
    heavy = (e - heavy_core) == 0
    away = (e - heavy_core) * (e - heavy_core)
    nch = most - away * (most - least)
    oth_nch = least + away * (most - least)

    barrier = pltpu.get_barrier_semaphore()
    for device in (to_p, to_x, to_y):
        pl.semaphore_signal(barrier, inc=1, device_id=device, device_id_type=MESH)

    def weight_copies():
        copies = []
        for s in range(4):
            copies.append(pltpu.make_async_copy(wg_hbm.at[s], wgu.at[0, s], wsem.at[0, s]))
            copies.append(pltpu.make_async_copy(wu_hbm.at[s], wgu.at[1, s], wsem.at[1, s]))
            there = wd_hbm.at[:, pl.ds(s * width, width)]
            copies.append(pltpu.make_async_copy(there, wd.at[s], wsem.at[2, s]))
        return copies

    for c in weight_copies():
        c.start()

    def rows(k):
        return pl.ds(pl.multiple_of(k * chunk, chunk), chunk)

    def first(k):
        return pl.ds(pl.multiple_of(k * chunk, hc), hc)

    def second(k):
        return pl.ds(pl.multiple_of(k * chunk + hc, hc), hc)

    def remote(kind, k, src, dst, device):
        return pltpu.make_async_remote_copy(
            src_ref=src,
            dst_ref=dst,
            send_sem=send_sem.at[kind, k],
            recv_sem=recv_sem.at[kind, k],
            device_id=device,
            device_id_type=MESH,
        )

    def ag1x(k):
        return remote(AG1X, k, xg.at[t, rows(k)], xg.at[t, rows(k)], to_x)

    def ag1y(k):
        return remote(AG1Y, k, xg.at[t, rows(k)], xg.at[t, rows(k)], to_y)

    def ag2x(k):
        return remote(AG2X, k, xg.at[ty, second(k)], xg.at[ty, second(k)], to_x)

    def ag2y(k):
        return remote(AG2Y, k, xg.at[tx, first(k)], xg.at[tx, first(k)], to_y)

    def rs1x(k):
        return remote(RS1X, k, snd.at[0, first(k)], got_d.at[first(k)], to_x)

    def rs1y(k):
        return remote(RS1Y, k, snd.at[0, second(k)], got_d.at[second(k)], to_y)

    def rs2x(k):
        return remote(RS2X, k, snd.at[1, rows(k)], got_x.at[rows(k)], to_x)

    def rs2y(k):
        return remote(RS2Y, k, snd.at[2, rows(k)], got_y.at[rows(k)], to_y)

    def give(k):
        return remote(RET, k, back.at[0, rows(k)], back.at[1, rows(k)], to_p)

    def hand(k):
        return remote(HAND, k, dsp.at[rows(k)], mrg.at[rows(k)], to_p)

    def each(count, act, start=0):
        def go(k, carry):
            act(k)
            return carry

        lax.fori_loop(start, count, go, 0)

    before = (
        lax.broadcasted_iota(jnp.int32, (tok_rows, tok_rows), 0)
        < lax.broadcasted_iota(jnp.int32, (tok_rows, tok_rows), 1)
    )
    before = jnp.where(before, 1.0, 0.0).astype(jnp.bfloat16)

    def onehot(expert, count, offset):
        named = (ids_ref[0:1, :] == expert) | (ids_ref[1:2, :] == expert)
        named = jnp.where(named, 1.0, 0.0)
        wide = jnp.broadcast_to(named, (16, tok_rows)).astype(jnp.bfloat16)
        pos = jnp.dot(wide, before, preferred_element_type=jnp.float32)[0:1, :]
        pos = jnp.where(named > 0.5, pos, -2.0 * tok_rows).astype(jnp.int32) + offset
        slot = lax.broadcasted_iota(jnp.int32, (count, tok_rows), 0)
        return jnp.where(slot == pos, 1.0, 0.0)

    def gate_column(expert):
        row = jnp.where(ids_ref[0:1, :] == expert, gat_ref[0:1, :], 0.0)
        row += jnp.where(ids_ref[1:2, :] == expert, gat_ref[1:2, :], 0.0)
        return jnp.broadcast_to(row, (8, tok_rows)).T[:, 0:1]

    def columns(c):
        return pl.ds(pl.multiple_of(c * tile, 128), tile)

    def ready(k):
        ag1x(k).start()
        ag1y(k).start()

    def merge(lo, hi):
        each(nch, lambda k: hand(k).wait_recv())
        xg[t, lo:hi] = xg[t, lo:hi] + mrg[lo:hi, :]

    pick_own = onehot(e, cap, 0)
    pick_own_b = pick_own.astype(jnp.bfloat16)

    @functools.partial(each, 3)
    def _(c):
        part = jnp.dot(pick_own_b, tok_ref[:, columns(c)], preferred_element_type=jnp.float32)
        xg[t, 0:cap, columns(c)] = part.astype(jnp.bfloat16)

    pl.semaphore_wait(barrier, 3)

    @pl.when(heavy)
    def _():
        each(ahead, ready)

    xg[t, cap:tok_rows] = jnp.zeros((tok_rows - cap, width), jnp.bfloat16)
    pick_oth = onehot(1 - e, tok_rows, off_ref[0:1, 0:1])
    pick_oth_b = pick_oth.astype(jnp.bfloat16)

    @functools.partial(each, 3)
    def _(c):
        part = jnp.dot(pick_oth_b, tok_ref[:, columns(c)], preferred_element_type=jnp.float32)
        dsp[:, columns(c)] = part.astype(jnp.bfloat16)

    each(oth_nch, lambda k: hand(k).start())
    pt_own[...] = pick_own.T.astype(jnp.bfloat16)
    pt_oth[...] = pick_oth.T.astype(jnp.bfloat16)

    @pl.when(heavy)
    def _():
        if light_rows < tok_rows:
            gap = tok_rows - light_rows
            back[1, light_rows:tok_rows] = jnp.zeros((gap, width), jnp.bfloat16)

    @pl.when(jnp.logical_not(heavy))
    def _():
        merge(0, light_rows)
        each(ahead, ready)

    def step(i, carry):
        @pl.when(heavy & (i + ahead == cap // chunk))
        def _():
            merge(cap, tok_rows)

        @pl.when(i + ahead < nch)
        def _():
            ready(i + ahead)

        @pl.when(i < nch)
        def _():
            ag1x(i).wait_recv()
            ag2y(i).start()
            ag1y(i).wait_recv()
            ag2x(i).start()

        @pl.when(i == 1)
        def _():
            for c in weight_copies():
                c.wait()

        @pl.when((i >= 1) & (i - 1 < nch))
        def _():
            k = i - 1
            ag2x(k).wait_recv()
            ag2y(k).wait_recv()
            acc[...] = jnp.zeros_like(acc)

            @functools.partial(each, 8)
            def _(n):
                s, j = n // 2, n % 2
                acc[j] += jnp.dot(xg[s, rows(k), :], wgu[j, s], preferred_element_type=jnp.float32)

            gate = acc[0]
            gated = (gate / (1.0 + jnp.exp(-gate)) * acc[1]).astype(jnp.bfloat16)

            @functools.partial(each, 3)
            def _(r):
                towards = td + (tx - td) * ((r + 1) // 2) + (ty - tx) * (r // 2)
                part = jnp.dot(gated, wd[towards], preferred_element_type=jnp.float32)
                snd[r, rows(k), :] = part.astype(jnp.bfloat16)

                @pl.when(r == 0)
                def _():
                    rs1x(k).start()
                    rs1y(k).start()

            own[rows(k), :] = jnp.dot(gated, wd[t], preferred_element_type=jnp.float32)

        @pl.when((i >= 2) & (i - 2 < nch))
        def _():
            k = i - 2
            rs1x(k).wait_recv()
            snd[2, first(k), :] = (
                snd[2, first(k), :].astype(jnp.float32) + got_d[first(k), :].astype(jnp.float32)
            ).astype(jnp.bfloat16)
            rs2y(k).start()
            rs1y(k).wait_recv()
            snd[1, second(k), :] = (
                snd[1, second(k), :].astype(jnp.float32) + got_d[second(k), :].astype(jnp.float32)
            ).astype(jnp.bfloat16)
            rs2x(k).start()

        @pl.when(i >= 3)
        def _():
            k = i - 3
            rs2x(k).wait_recv()
            rs2y(k).wait_recv()
            back[0, rows(k), :] = (
                own[rows(k), :]
                + got_x[rows(k), :].astype(jnp.float32)
                + got_y[rows(k), :].astype(jnp.float32)
            ).astype(jnp.bfloat16)
            give(k).start()

        return carry

    lax.fori_loop(0, nch + 3, step, 0)

    each(oth_nch, lambda k: give(k).wait_recv())
    weight_own, weight_oth = gate_column(e), gate_column(1 - e)

    @functools.partial(each, 3)
    def _(c):
        mine = jnp.dot(
            pt_own[...], back[0, 0:cap, columns(c)], preferred_element_type=jnp.float32
        )
        theirs = jnp.dot(pt_oth[...], back[1, :, columns(c)], preferred_element_type=jnp.float32)
        out_ref[:, columns(c)] = (weight_own * mine + weight_oth * theirs).astype(jnp.bfloat16)

    def drain(k):
        for make in (ag1x, ag1y, ag2x, ag2y, rs1x, rs1y, rs2x, rs2y, give):
            make(k).wait_send()

    each(nch, drain)
    each(oth_nch, lambda k: hand(k).wait_send())


def moe_call(heavy_core, light_rows, number, tokens, ids, gates, offset, w_gate, w_up, w_down):
    tok_rows, width = tokens.shape
    tensor, _, hidden = w_gate.shape
    chunk = tok_rows // 8
    bf16 = jnp.bfloat16
    vmem = pl.BlockSpec(memory_space=pltpu.VMEM)
    hbm = pl.BlockSpec(memory_space=pl.ANY)
    return pl.pallas_call(
        functools.partial(moe_kernel, heavy_core, light_rows, chunk, 3),
        out_shape=jax.ShapeDtypeStruct((tok_rows, width), bf16),
        in_specs=[vmem, vmem, vmem, vmem, hbm, hbm, hbm],
        out_specs=vmem,
        scratch_shapes=[
            pltpu.VMEM((tensor, tok_rows, width), bf16),
            pltpu.VMEM((2, tensor, width, hidden), bf16),
            pltpu.VMEM((tensor, hidden, width), bf16),
            pltpu.VMEM((tok_rows, width), bf16),
            pltpu.VMEM((tok_rows, width), bf16),
            pltpu.VMEM((2, chunk, hidden), jnp.float32),
            pltpu.VMEM((3, tok_rows, width), bf16),
            pltpu.VMEM((tok_rows, width), bf16),
            pltpu.VMEM((tok_rows, width), bf16),
            pltpu.VMEM((tok_rows, width), bf16),
            pltpu.VMEM((tok_rows, width), jnp.float32),
            pltpu.VMEM((2, tok_rows, width), bf16),
            pltpu.VMEM((tok_rows, tok_rows // 2), bf16),
            pltpu.VMEM((tok_rows, tok_rows), bf16),
            pltpu.SemaphoreType.DMA((10, 8)),
            pltpu.SemaphoreType.DMA((10, 8)),
            pltpu.SemaphoreType.DMA((3, 4)),
        ],
        compiler_params=pltpu.CompilerParams(
            collective_id=number, has_side_effects=True, vmem_limit_bytes=60 * 1024 * 1024
        ),
        cost_estimate=pl.CostEstimate(
            flops=6 * tok_rows * tensor * width * hidden,
            bytes_accessed=6 * tensor * width * hidden,
            transcendentals=0,
        ),
    )(tokens, ids, gates, offset, w_gate, w_up, w_down)


def fused(tokens, route_ids, route_gates, w_gate, w_up, w_down):
    tok_rows, width = tokens.shape
    tensor = lax.axis_size("tensor")
    hidden = w_gate.shape[2]
    e = lax.axis_index("expert")
    ids, gates = route_ids.T, route_gates.T
    counts = jnp.sum(
        (ids[:, :, None] == jnp.arange(2, dtype=jnp.int32)).astype(jnp.int32), axis=(0, 1)
    )
    theirs = lax.ppermute(counts, "expert", [(0, 1), (1, 0)])
    totals = counts + theirs
    offset = jnp.broadcast_to(jnp.where(e == 0, theirs[1], theirs[0]), (8, 128))
    sizes = (tok_rows // 2, tok_rows * 5 // 8)
    plans = [(core, size) for size in sizes + (tok_rows,) for core in range(2)]
    least = jnp.min(totals)
    level = sum((least > s).astype(jnp.int32) for s in sizes)
    heavy = (totals[1] > totals[0]).astype(jnp.int32)
    index = 2 * level + heavy
    branches = [functools.partial(moe_call, *plan, n) for n, plan in enumerate(plans)]
    return lax.switch(
        index,
        branches,
        tokens,
        ids,
        gates,
        offset,
        w_gate.reshape(tensor, width, hidden),
        w_up.reshape(tensor, width, hidden),
        w_down.reshape(hidden, tensor * width),
    )


def general(tokens, route_ids, route_gates, w_gate, w_up, w_down):
    tok_rows, width_dev = tokens.shape
    picks = route_ids.shape[1]
    n_source = lax.axis_size("expert")
    local_count = w_gate.shape[0]
    n_flight = n_source * local_count
    capacity = tok_rows // 2
    flat_ids = route_ids.reshape(-1)
    onehot = (flat_ids[:, None] == jnp.arange(n_flight, dtype=jnp.int32)[None, :]).astype(jnp.int32)
    earlier = jnp.cumsum(onehot, axis=0) - onehot
    position = jnp.sum(earlier * onehot, axis=1)
    in_window = flat_ids < n_flight
    slots = jnp.where(in_window, flat_ids * capacity + position, n_flight * capacity)
    repeated = jnp.repeat(tokens, picks, axis=0)
    buffer = (
        jnp.zeros((n_flight * capacity, width_dev), jnp.bfloat16)
        .at[slots]
        .set(repeated, mode="drop")
    )
    buffer = buffer.reshape(n_flight, capacity, width_dev)
    received = lax.all_to_all(buffer, "expert", split_axis=0, concat_axis=0, tiled=True)
    piece = lax.all_gather(received, "tensor", axis=2, tiled=True)
    columns = piece.shape[2]
    grouped = piece.reshape(n_source, local_count, capacity, columns)
    gate = jnp.einsum("secd,edf->secf", grouped, w_gate, preferred_element_type=jnp.float32)
    upper = jnp.einsum("secd,edf->secf", grouped, w_up, preferred_element_type=jnp.float32)
    gated = (jax.nn.silu(gate) * upper).astype(jnp.bfloat16)
    partial_out = jnp.einsum("secf,efd->secd", gated, w_down, preferred_element_type=jnp.float32)
    partial_out = partial_out.reshape(n_flight, capacity, partial_out.shape[3])
    summed = lax.psum_scatter(partial_out, "tensor", scatter_dimension=2, tiled=True)
    expert_out = summed.astype(jnp.bfloat16)
    back = lax.all_to_all(expert_out, "expert", split_axis=0, concat_axis=0, tiled=True)
    flat_back = back.reshape(n_flight * capacity, width_dev)
    picked = jnp.take(flat_back, slots, axis=0, mode="fill", fill_value=0).astype(jnp.float32)
    picked = picked.reshape(tok_rows, picks, width_dev)
    mixed = jnp.sum(picked * route_gates[:, :, None], axis=1)
    return mixed.astype(jnp.bfloat16)


def solution(mesh):
    placed = (
        P(("dp", "expert"), "tensor"),
        P(("dp", "expert"), None),
        P(("dp", "expert"), None),
        P("expert", None, "tensor"),
        P("expert", None, "tensor"),
        P("expert", "tensor", None),
    )
    square = mesh.shape["tensor"] == 4 and mesh.shape["expert"] == 2
    return jax.shard_map(
        fused if square else general,
        mesh=mesh,
        in_specs=placed,
        out_specs=P(("dp", "expert"), "tensor"),
        check_vma=False,
    )
```

```python
import functools

import jax
import jax.numpy as jnp
from jax import lax
from jax.experimental import pallas as pl
from jax.experimental.pallas import tpu as pltpu
from jax.sharding import PartitionSpec as P

MESH = pl.DeviceIdType.MESH
AG1X, AG1Y, AG2X, AG2Y, RS1X, RS1Y, RS2X, RS2Y, RET, HAND = range(10)


def moe_kernel(
    heavy_core,
    light_rows,
    chunk,
    ahead,
    tok_ref,
    ids_ref,
    gat_ref,
    their_ids_ref,
    wg_hbm,
    wu_hbm,
    wd_hbm,
    out_ref,
    xg,
    wgu,
    wd,
    dsp,
    mrg,
    acc,
    snd,
    got_d,
    got_x,
    got_y,
    own,
    back,
    pt_own,
    pt_oth,
    send_sem,
    recv_sem,
    wsem,
):
    tok_rows, width = tok_ref.shape
    hidden = wgu.shape[3]
    cap = tok_rows // 2
    hc = chunk // 2
    tile = width // 3
    e = lax.axis_index("expert")
    t = lax.axis_index("tensor")
    tx = (t // 2) * 2 + (1 - t % 2)
    ty = (1 - t // 2) * 2 + t % 2
    td = 3 - t
    to_x, to_y, to_p = {"tensor": tx}, {"tensor": ty}, {"expert": 1 - e}
    most, least = tok_rows // chunk, light_rows // chunk
    heavy = (e - heavy_core) == 0
    away = (e - heavy_core) * (e - heavy_core)
    nch = most - away * (most - least)
    steps = (nch + 1) // 2
    block = 2 * chunk
    oth_nch = least + away * (most - least)

    barrier = pltpu.get_barrier_semaphore()
    for device in (to_p, to_x, to_y):
        pl.semaphore_signal(barrier, inc=1, device_id=device, device_id_type=MESH)

    def weight_copies():
        copies = []
        for s in range(4):
            copies.append(pltpu.make_async_copy(wg_hbm.at[s], wgu.at[0, s], wsem.at[0, s]))
            copies.append(pltpu.make_async_copy(wu_hbm.at[s], wgu.at[1, s], wsem.at[1, s]))
            there = wd_hbm.at[:, pl.ds(s * width, width)]
            copies.append(pltpu.make_async_copy(there, wd.at[s], wsem.at[2, s]))
        return copies

    for c in weight_copies():
        c.start()

    def rows(k):
        return pl.ds(pl.multiple_of(k * chunk, chunk), chunk)

    def first(k):
        return pl.ds(pl.multiple_of(k * chunk, hc), hc)

    def second(k):
        return pl.ds(pl.multiple_of(k * chunk + hc, hc), hc)

    def remote(kind, k, src, dst, device):
        return pltpu.make_async_remote_copy(
            src_ref=src,
            dst_ref=dst,
            send_sem=send_sem.at[kind, k],
            recv_sem=recv_sem.at[kind, k],
            device_id=device,
            device_id_type=MESH,
        )

    def ag1x(k):
        return remote(AG1X, k, xg.at[t, rows(k)], xg.at[t, rows(k)], to_x)

    def ag1y(k):
        return remote(AG1Y, k, xg.at[t, rows(k)], xg.at[t, rows(k)], to_y)

    def ag2x(k):
        return remote(AG2X, k, xg.at[ty, second(k)], xg.at[ty, second(k)], to_x)

    def ag2y(k):
        return remote(AG2Y, k, xg.at[tx, first(k)], xg.at[tx, first(k)], to_y)

    def rs1x(k):
        return remote(RS1X, k, snd.at[0, first(k)], got_d.at[first(k)], to_x)

    def rs1y(k):
        return remote(RS1Y, k, snd.at[0, second(k)], got_d.at[second(k)], to_y)

    def rs2x(k):
        return remote(RS2X, k, snd.at[1, rows(k)], got_x.at[rows(k)], to_x)

    def rs2y(k):
        return remote(RS2Y, k, snd.at[2, rows(k)], got_y.at[rows(k)], to_y)

    def give(k):
        return remote(RET, k, back.at[0, rows(k)], back.at[1, rows(k)], to_p)

    def hand(k):
        return remote(HAND, k, dsp.at[rows(k)], mrg.at[rows(k)], to_p)

    def each(count, act, start=0):
        def go(k, carry):
            act(k)
            return carry

        lax.fori_loop(start, count, go, 0)

    before = (
        lax.broadcasted_iota(jnp.int32, (tok_rows, tok_rows), 0)
        < lax.broadcasted_iota(jnp.int32, (tok_rows, tok_rows), 1)
    )
    before = jnp.where(before, 1.0, 0.0).astype(jnp.bfloat16)

    def onehot(expert, count, offset):
        named = (ids_ref[0:1, :] == expert) | (ids_ref[1:2, :] == expert)
        named = jnp.where(named, 1.0, 0.0)
        wide = jnp.broadcast_to(named, (16, tok_rows)).astype(jnp.bfloat16)
        pos = jnp.dot(wide, before, preferred_element_type=jnp.float32)[0:1, :]
        pos = jnp.where(named > 0.5, pos, -2.0 * tok_rows).astype(jnp.int32) + offset
        slot = lax.broadcasted_iota(jnp.int32, (count, tok_rows), 0)
        return jnp.where(slot == pos, 1.0, 0.0)

    def gate_column(expert):
        row = jnp.where(ids_ref[0:1, :] == expert, gat_ref[0:1, :], 0.0)
        row += jnp.where(ids_ref[1:2, :] == expert, gat_ref[1:2, :], 0.0)
        return jnp.broadcast_to(row, (8, tok_rows)).T[:, 0:1]

    def columns(c):
        return pl.ds(pl.multiple_of(c * tile, 128), tile)

    def pieces(k, act):
        for p in (2 * k, 2 * k + 1):
            pl.when((p >= 0) & (p < nch))(functools.partial(act, p))

    def block_rows(k):
        return pl.ds(pl.multiple_of(k * block, block), block)

    def send_piece(p):
        ag1x(p).start()
        ag1y(p).start()

    def forward_piece(p):
        ag1x(p).wait_recv()
        ag2y(p).start()
        ag1y(p).wait_recv()
        ag2x(p).start()

    def gathered_piece(p):
        ag2x(p).wait_recv()
        ag2y(p).wait_recv()

    def reduce_piece(p):
        rs1x(p).start()
        rs1y(p).start()

    def add_piece(p):
        rs1x(p).wait_recv()
        snd[2, first(p), :] = (
            snd[2, first(p), :].astype(jnp.float32) + got_d[first(p), :].astype(jnp.float32)
        ).astype(jnp.bfloat16)
        rs2y(p).start()
        rs1y(p).wait_recv()
        snd[1, second(p), :] = (
            snd[1, second(p), :].astype(jnp.float32) + got_d[second(p), :].astype(jnp.float32)
        ).astype(jnp.bfloat16)
        rs2x(p).start()

    def finish_piece(p):
        rs2x(p).wait_recv()
        rs2y(p).wait_recv()
        back[0, rows(p), :] = (
            own[rows(p), :]
            + got_x[rows(p), :].astype(jnp.float32)
            + got_y[rows(p), :].astype(jnp.float32)
        ).astype(jnp.bfloat16)
        give(p).start()

    def ready(k):
        pieces(k, send_piece)

    def merge(lo, hi):
        each(nch, lambda k: hand(k).wait_recv())
        xg[t, lo:hi] = xg[t, lo:hi] + mrg[lo:hi, :]

    pick_own = onehot(e, cap, 0)
    pick_own_b = pick_own.astype(jnp.bfloat16)

    @functools.partial(each, 3)
    def _(c):
        part = jnp.dot(pick_own_b, tok_ref[:, columns(c)], preferred_element_type=jnp.float32)
        xg[t, 0:cap, columns(c)] = part.astype(jnp.bfloat16)

    pl.semaphore_wait(barrier, 3)

    @pl.when(heavy)
    def _():
        each(ahead, ready)

    xg[t, cap:tok_rows] = jnp.zeros((tok_rows - cap, width), jnp.bfloat16)
    theirs_first = jnp.where(their_ids_ref[...] == 1 - e, 1.0, 0.0)
    offset = jnp.sum(jnp.sum(theirs_first, axis=1, keepdims=True), axis=0, keepdims=True)
    pick_oth = onehot(1 - e, tok_rows, offset.astype(jnp.int32))
    pick_oth_b = pick_oth.astype(jnp.bfloat16)

    @functools.partial(each, 3)
    def _(c):
        part = jnp.dot(pick_oth_b, tok_ref[:, columns(c)], preferred_element_type=jnp.float32)
        dsp[:, columns(c)] = part.astype(jnp.bfloat16)

    each(oth_nch, lambda k: hand(k).start())
    pt_own[...] = pick_own.T.astype(jnp.bfloat16)
    pt_oth[...] = pick_oth.T.astype(jnp.bfloat16)

    @pl.when(heavy)
    def _():
        if light_rows < tok_rows:
            gap = tok_rows - light_rows
            back[1, light_rows:tok_rows] = jnp.zeros((gap, width), jnp.bfloat16)

    @pl.when(jnp.logical_not(heavy))
    def _():
        merge(0, light_rows)
        each(ahead, ready)

    def step(i, carry):
        @pl.when(heavy & (i + ahead == cap // block))
        def _():
            merge(cap, tok_rows)

        ready(i + ahead)
        pieces(i, forward_piece)

        @pl.when(i == 1)
        def _():
            for c in weight_copies():
                c.wait()

        @pl.when((i >= 1) & (i - 1 < steps))
        def _():
            k = i - 1
            pieces(k, gathered_piece)
            acc[...] = jnp.zeros_like(acc)

            @functools.partial(each, 8)
            def _(n):
                s, j = n // 2, n % 2
                acc[j] += jnp.dot(
                    xg[s, block_rows(k), :], wgu[j, s], preferred_element_type=jnp.float32
                )

            gate = acc[0]
            gated = (gate / (1.0 + jnp.exp(-gate)) * acc[1]).astype(jnp.bfloat16)

            @functools.partial(each, 3)
            def _(r):
                towards = td + (tx - td) * ((r + 1) // 2) + (ty - tx) * (r // 2)
                part = jnp.dot(gated, wd[towards], preferred_element_type=jnp.float32)
                snd[r, block_rows(k), :] = part.astype(jnp.bfloat16)

                @pl.when(r == 0)
                def _():
                    pieces(k, reduce_piece)

            own[block_rows(k), :] = jnp.dot(gated, wd[t], preferred_element_type=jnp.float32)

        pieces(i - 2, add_piece)
        pieces(i - 3, finish_piece)
        return carry

    lax.fori_loop(0, steps + 3, step, 0)

    each(oth_nch, lambda k: give(k).wait_recv())
    weight_own, weight_oth = gate_column(e), gate_column(1 - e)

    @functools.partial(each, 3)
    def _(c):
        mine = jnp.dot(
            pt_own[...], back[0, 0:cap, columns(c)], preferred_element_type=jnp.float32
        )
        theirs = jnp.dot(pt_oth[...], back[1, :, columns(c)], preferred_element_type=jnp.float32)
        out_ref[:, columns(c)] = (weight_own * mine + weight_oth * theirs).astype(jnp.bfloat16)

    def drain(k):
        for make in (ag1x, ag1y, ag2x, ag2y, rs1x, rs1y, rs2x, rs2y, give):
            make(k).wait_send()

    each(nch, drain)
    each(oth_nch, lambda k: hand(k).wait_send())


def moe_call(heavy_core, light_rows, number, tokens, ids, gates, their_ids, w_gate, w_up, w_down):
    tok_rows, width = tokens.shape
    tensor, _, hidden = w_gate.shape
    chunk = tok_rows // 8
    bf16 = jnp.bfloat16
    vmem = pl.BlockSpec(memory_space=pltpu.VMEM)
    hbm = pl.BlockSpec(memory_space=pl.ANY)
    return pl.pallas_call(
        functools.partial(moe_kernel, heavy_core, light_rows, chunk, 2),
        out_shape=jax.ShapeDtypeStruct((tok_rows, width), bf16),
        in_specs=[vmem, vmem, vmem, vmem, hbm, hbm, hbm],
        out_specs=vmem,
        scratch_shapes=[
            pltpu.VMEM((tensor, tok_rows, width), bf16),
            pltpu.VMEM((2, tensor, width, hidden), bf16),
            pltpu.VMEM((tensor, hidden, width), bf16),
            pltpu.VMEM((tok_rows, width), bf16),
            pltpu.VMEM((tok_rows, width), bf16),
            pltpu.VMEM((2, 2 * chunk, hidden), jnp.float32),
            pltpu.VMEM((3, tok_rows, width), bf16),
            pltpu.VMEM((tok_rows, width), bf16),
            pltpu.VMEM((tok_rows, width), bf16),
            pltpu.VMEM((tok_rows, width), bf16),
            pltpu.VMEM((tok_rows, width), jnp.float32),
            pltpu.VMEM((2, tok_rows, width), bf16),
            pltpu.VMEM((tok_rows, tok_rows // 2), bf16),
            pltpu.VMEM((tok_rows, tok_rows), bf16),
            pltpu.SemaphoreType.DMA((10, 8)),
            pltpu.SemaphoreType.DMA((10, 8)),
            pltpu.SemaphoreType.DMA((3, 4)),
        ],
        compiler_params=pltpu.CompilerParams(
            collective_id=number, has_side_effects=True, vmem_limit_bytes=60 * 1024 * 1024
        ),
        cost_estimate=pl.CostEstimate(
            flops=6 * tok_rows * tensor * width * hidden,
            bytes_accessed=6 * tensor * width * hidden,
            transcendentals=0,
        ),
    )(tokens, ids, gates, their_ids, w_gate, w_up, w_down)


def fused(tokens, route_ids, route_gates, w_gate, w_up, w_down):
    tok_rows, width = tokens.shape
    tensor = lax.axis_size("tensor")
    hidden = w_gate.shape[2]
    ids, gates = route_ids.T, route_gates.T
    their_ids = lax.ppermute(ids, "expert", [(0, 1), (1, 0)])
    unit = 4 * tok_rows

    def tally(names):
        return jnp.where(names == 0, 1, 0) + jnp.where(names == 1, unit, 0)

    both = jnp.sum(tally(ids) + tally(their_ids))
    total_0, total_1 = both % unit, both // unit
    sizes = (tok_rows // 2, tok_rows * 5 // 8)
    plans = [(core, size) for size in sizes + (tok_rows,) for core in range(2)]
    least = jnp.minimum(total_0, total_1)
    level = sum((least > s).astype(jnp.int32) for s in sizes)
    heavy = (total_1 > total_0).astype(jnp.int32)
    index = 2 * level + heavy
    branches = [functools.partial(moe_call, *plan, n) for n, plan in enumerate(plans)]
    return lax.switch(
        index,
        branches,
        tokens,
        ids,
        gates,
        their_ids,
        w_gate.reshape(tensor, width, hidden),
        w_up.reshape(tensor, width, hidden),
        w_down.reshape(hidden, tensor * width),
    )


def general(tokens, route_ids, route_gates, w_gate, w_up, w_down):
    tok_rows, width_dev = tokens.shape
    picks = route_ids.shape[1]
    n_source = lax.axis_size("expert")
    local_count = w_gate.shape[0]
    n_flight = n_source * local_count
    capacity = tok_rows // 2
    flat_ids = route_ids.reshape(-1)
    onehot = (flat_ids[:, None] == jnp.arange(n_flight, dtype=jnp.int32)[None, :]).astype(jnp.int32)
    earlier = jnp.cumsum(onehot, axis=0) - onehot
    position = jnp.sum(earlier * onehot, axis=1)
    in_window = flat_ids < n_flight
    slots = jnp.where(in_window, flat_ids * capacity + position, n_flight * capacity)
    repeated = jnp.repeat(tokens, picks, axis=0)
    buffer = (
        jnp.zeros((n_flight * capacity, width_dev), jnp.bfloat16)
        .at[slots]
        .set(repeated, mode="drop")
    )
    buffer = buffer.reshape(n_flight, capacity, width_dev)
    received = lax.all_to_all(buffer, "expert", split_axis=0, concat_axis=0, tiled=True)
    piece = lax.all_gather(received, "tensor", axis=2, tiled=True)
    columns = piece.shape[2]
    grouped = piece.reshape(n_source, local_count, capacity, columns)
    gate = jnp.einsum("secd,edf->secf", grouped, w_gate, preferred_element_type=jnp.float32)
    upper = jnp.einsum("secd,edf->secf", grouped, w_up, preferred_element_type=jnp.float32)
    gated = (jax.nn.silu(gate) * upper).astype(jnp.bfloat16)
    partial_out = jnp.einsum("secf,efd->secd", gated, w_down, preferred_element_type=jnp.float32)
    partial_out = partial_out.reshape(n_flight, capacity, partial_out.shape[3])
    summed = lax.psum_scatter(partial_out, "tensor", scatter_dimension=2, tiled=True)
    expert_out = summed.astype(jnp.bfloat16)
    back = lax.all_to_all(expert_out, "expert", split_axis=0, concat_axis=0, tiled=True)
    flat_back = back.reshape(n_flight * capacity, width_dev)
    picked = jnp.take(flat_back, slots, axis=0, mode="fill", fill_value=0).astype(jnp.float32)
    picked = picked.reshape(tok_rows, picks, width_dev)
    mixed = jnp.sum(picked * route_gates[:, :, None], axis=1)
    return mixed.astype(jnp.bfloat16)


def solution(mesh):
    placed = (
        P(("dp", "expert"), "tensor"),
        P(("dp", "expert"), None),
        P(("dp", "expert"), None),
        P("expert", None, "tensor"),
        P("expert", None, "tensor"),
        P("expert", "tensor", None),
    )
    square = mesh.shape["tensor"] == 4 and mesh.shape["expert"] == 2
    return jax.shard_map(
        fused if square else general,
        mesh=mesh,
        in_specs=placed,
        out_specs=P(("dp", "expert"), "tensor"),
        check_vma=False,
    )
```

```python
import functools

import jax
import jax.numpy as jnp
from jax import lax
from jax.experimental import pallas as pl
from jax.experimental.pallas import tpu as pltpu
from jax.sharding import PartitionSpec as P

MESH = pl.DeviceIdType.MESH
AG1X, AG1Y, AG2X, AG2Y, RS1X, RS1Y, RS2X, RS2Y, RET, HAND = range(10)


def moe_kernel(
    heavy_core,
    light_rows,
    chunk,
    ahead,
    tok_ref,
    ids_ref,
    gat_ref,
    their_ids_ref,
    wg_hbm,
    wu_hbm,
    wd_hbm,
    out_ref,
    xg,
    wgu,
    wd,
    dsp,
    mrg,
    acc,
    snd,
    got_d,
    got_x,
    got_y,
    own,
    back,
    pt_own,
    pt_oth,
    send_sem,
    recv_sem,
    wsem,
):
    tok_rows, width = tok_ref.shape
    hidden = wgu.shape[3]
    cap = tok_rows // 2
    hc = chunk // 2
    tile = width // 3
    e = lax.axis_index("expert")
    t = lax.axis_index("tensor")
    tx = (t // 2) * 2 + (1 - t % 2)
    ty = (1 - t // 2) * 2 + t % 2
    td = 3 - t
    to_x, to_y, to_p = {"tensor": tx}, {"tensor": ty}, {"expert": 1 - e}
    most, least = tok_rows // chunk, light_rows // chunk
    heavy = (e - heavy_core) == 0
    light = jnp.logical_not(heavy)
    away = (e - heavy_core) * (e - heavy_core)
    nch = most - away * (most - least)
    per = 4
    block = per * chunk
    steps = (nch + per - 1) // per
    half = cap // chunk
    hand_from, hand_to = away * half, least + away * (most - least)
    got_from, got_to = half - away * half, most - away * (most - least)
    give_from = half - away * half
    take_from = away * half
    oth_nch = least + away * (most - least)

    barrier = pltpu.get_barrier_semaphore()
    for device in (to_p, to_x, to_y):
        pl.semaphore_signal(barrier, inc=1, device_id=device, device_id_type=MESH)

    def weight_copies():
        copies = []
        for s in range(4):
            copies.append(pltpu.make_async_copy(wg_hbm.at[s], wgu.at[0, s], wsem.at[0, s]))
            copies.append(pltpu.make_async_copy(wu_hbm.at[s], wgu.at[1, s], wsem.at[1, s]))
            there = wd_hbm.at[:, pl.ds(s * width, width)]
            copies.append(pltpu.make_async_copy(there, wd.at[s], wsem.at[2, s]))
        return copies

    for c in weight_copies():
        c.start()

    def rows(k):
        return pl.ds(pl.multiple_of(k * chunk, chunk), chunk)

    def first(k):
        return pl.ds(pl.multiple_of(k * chunk, hc), hc)

    def second(k):
        return pl.ds(pl.multiple_of(k * chunk + hc, hc), hc)

    def remote(kind, k, src, dst, device):
        return pltpu.make_async_remote_copy(
            src_ref=src,
            dst_ref=dst,
            send_sem=send_sem.at[kind, k],
            recv_sem=recv_sem.at[kind, k],
            device_id=device,
            device_id_type=MESH,
        )

    def ag1x(k):
        return remote(AG1X, k, xg.at[t, rows(k)], xg.at[t, rows(k)], to_x)

    def ag1y(k):
        return remote(AG1Y, k, xg.at[t, rows(k)], xg.at[t, rows(k)], to_y)

    def ag2x(k):
        return remote(AG2X, k, xg.at[ty, second(k)], xg.at[ty, second(k)], to_x)

    def ag2y(k):
        return remote(AG2Y, k, xg.at[tx, first(k)], xg.at[tx, first(k)], to_y)

    def rs1x(k):
        return remote(RS1X, k, snd.at[0, first(k)], got_d.at[first(k)], to_x)

    def rs1y(k):
        return remote(RS1Y, k, snd.at[0, second(k)], got_d.at[second(k)], to_y)

    def rs2x(k):
        return remote(RS2X, k, snd.at[1, rows(k)], got_x.at[rows(k)], to_x)

    def rs2y(k):
        return remote(RS2Y, k, snd.at[2, rows(k)], got_y.at[rows(k)], to_y)

    def give(k):
        return remote(RET, k, back.at[0, rows(k)], back.at[1, rows(k)], to_p)

    def hand_light(k):
        return remote(HAND, k, dsp.at[rows(k)], mrg.at[rows(k)], to_p)

    def hand_heavy(k):
        return remote(HAND, k, dsp.at[rows(k)], xg.at[t, rows(k)], to_p)

    def each(count, act, start=0):
        def go(k, carry):
            act(k)
            return carry

        lax.fori_loop(start, count, go, 0)

    before = (
        lax.broadcasted_iota(jnp.int32, (tok_rows, tok_rows), 0)
        < lax.broadcasted_iota(jnp.int32, (tok_rows, tok_rows), 1)
    )
    before = jnp.where(before, 1.0, 0.0).astype(jnp.bfloat16)

    def onehot(expert, count, offset):
        named = (ids_ref[0:1, :] == expert) | (ids_ref[1:2, :] == expert)
        named = jnp.where(named, 1.0, 0.0)
        wide = jnp.broadcast_to(named, (16, tok_rows)).astype(jnp.bfloat16)
        pos = jnp.dot(wide, before, preferred_element_type=jnp.float32)[0:1, :]
        pos = jnp.where(named > 0.5, pos, -2.0 * tok_rows).astype(jnp.int32) + offset
        slot = lax.broadcasted_iota(jnp.int32, (count, tok_rows), 0)
        return jnp.where(slot == pos, 1.0, 0.0)

    def gate_column(expert):
        row = jnp.where(ids_ref[0:1, :] == expert, gat_ref[0:1, :], 0.0)
        row += jnp.where(ids_ref[1:2, :] == expert, gat_ref[1:2, :], 0.0)
        return jnp.broadcast_to(row, (8, tok_rows)).T[:, 0:1]

    def columns(c):
        return pl.ds(pl.multiple_of(c * tile, 128), tile)

    def pieces(k, act):
        def go(j, carry):
            p = per * k + j
            pl.when((p >= 0) & (p < nch))(functools.partial(act, p))
            return carry

        lax.fori_loop(0, per, go, 0)

    def block_rows(k):
        return pl.ds(pl.multiple_of(k * block, block), block)

    def send_piece(p):
        ag1x(p).start()
        ag1y(p).start()

    def forward_piece(p):
        ag1x(p).wait_recv()
        ag2y(p).start()
        ag1y(p).wait_recv()
        ag2x(p).start()

    def gathered_piece(p):
        ag2x(p).wait_recv()
        ag2y(p).wait_recv()

    def reduce_piece(p):
        rs1x(p).start()
        rs1y(p).start()

    def add_piece(p):
        rs1x(p).wait_recv()
        snd[2, first(p), :] = (
            snd[2, first(p), :].astype(jnp.float32) + got_d[first(p), :].astype(jnp.float32)
        ).astype(jnp.bfloat16)
        rs2y(p).start()
        rs1y(p).wait_recv()
        snd[1, second(p), :] = (
            snd[1, second(p), :].astype(jnp.float32) + got_d[second(p), :].astype(jnp.float32)
        ).astype(jnp.bfloat16)
        rs2x(p).start()

    def finish_piece(p):
        rs2x(p).wait_recv()
        rs2y(p).wait_recv()
        back[0, rows(p), :] = (
            own[rows(p), :]
            + got_x[rows(p), :].astype(jnp.float32)
            + got_y[rows(p), :].astype(jnp.float32)
        ).astype(jnp.bfloat16)

        @pl.when(p >= give_from)
        def _():
            give(p).start()

    def ready(k):
        pieces(k, send_piece)

    pick_own = onehot(e, cap, 0)
    pick_own_b = pick_own.astype(jnp.bfloat16)

    @functools.partial(each, 3)
    def _(c):
        part = jnp.dot(pick_own_b, tok_ref[:, columns(c)], preferred_element_type=jnp.float32)
        xg[t, 0:cap, columns(c)] = part.astype(jnp.bfloat16)

    pl.semaphore_wait(barrier, 3)

    @pl.when(heavy)
    def _():
        each(ahead, ready)

    theirs_first = jnp.where(their_ids_ref[...] == 1 - e, 1.0, 0.0)
    offset = jnp.sum(jnp.sum(theirs_first, axis=1, keepdims=True), axis=0, keepdims=True)
    pick_oth = onehot(1 - e, tok_rows, offset.astype(jnp.int32))
    pick_oth_b = pick_oth.astype(jnp.bfloat16)

    def hand_over(lo, hi, hand):
        @functools.partial(each, 3)
        def _(c):
            part = jnp.dot(
                pick_oth_b[lo:hi], tok_ref[:, columns(c)], preferred_element_type=jnp.float32
            )
            dsp[lo:hi, columns(c)] = part.astype(jnp.bfloat16)

        each(hand_to, lambda k: hand(k).start(), hand_from)

    @pl.when(heavy)
    def _():
        hand_over(0, light_rows, hand_light)

    @pl.when(light)
    def _():
        hand_over(cap, tok_rows, hand_heavy)

    pt_own[...] = pick_own.T.astype(jnp.bfloat16)
    pt_oth[...] = pick_oth.T.astype(jnp.bfloat16)

    @pl.when(light)
    def _():
        each(got_to, lambda k: hand_light(k).wait_recv(), got_from)
        xg[t, 0:cap] = xg[t, 0:cap] + mrg[0:cap, :]
        if light_rows > cap:
            xg[t, cap:light_rows] = mrg[cap:light_rows, :]
        each(ahead, ready)

    def step(i, carry):
        @pl.when(heavy & (i + ahead == cap // block))
        def _():
            each(got_to, lambda k: hand_heavy(k).wait_recv(), got_from)

        ready(i + ahead)
        pieces(i, forward_piece)

        @pl.when(i == 1)
        def _():
            for c in weight_copies():
                c.wait()

        @pl.when((i >= 1) & (i - 1 < steps))
        def _():
            k = i - 1
            pieces(k, gathered_piece)
            acc[...] = jnp.zeros_like(acc)

            @functools.partial(each, 8)
            def _(n):
                s, j = n // 2, n % 2
                acc[j] += jnp.dot(
                    xg[s, block_rows(k), :], wgu[j, s], preferred_element_type=jnp.float32
                )

            gate = acc[0]
            gated = (gate / (1.0 + jnp.exp(-gate)) * acc[1]).astype(jnp.bfloat16)

            @functools.partial(each, 3)
            def _(r):
                towards = td + (tx - td) * ((r + 1) // 2) + (ty - tx) * (r // 2)
                part = jnp.dot(gated, wd[towards], preferred_element_type=jnp.float32)
                snd[r, block_rows(k), :] = part.astype(jnp.bfloat16)

                @pl.when(r == 0)
                def _():
                    pieces(k, reduce_piece)

            own[block_rows(k), :] = jnp.dot(gated, wd[t], preferred_element_type=jnp.float32)

        pieces(i - 2, add_piece)
        pieces(i - 3, finish_piece)
        return carry

    lax.fori_loop(0, steps + 3, step, 0)

    weight_own, weight_oth = gate_column(e), gate_column(1 - e)

    @functools.partial(each, 3)
    def _(c):
        mine = jnp.dot(
            pt_own[...], back[0, 0:cap, columns(c)], preferred_element_type=jnp.float32
        )
        own[:, columns(c)] = weight_own * mine

    each(oth_nch, lambda k: give(k).wait_recv(), take_from)

    def combine(lo, hi):
        @functools.partial(each, 3)
        def _(c):
            theirs = jnp.dot(
                pt_oth[:, lo:hi], back[1, lo:hi, columns(c)], preferred_element_type=jnp.float32
            )
            out_ref[:, columns(c)] = (own[:, columns(c)] + weight_oth * theirs).astype(
                jnp.bfloat16
            )

    @pl.when(heavy)
    def _():
        combine(0, light_rows)

    @pl.when(light)
    def _():
        combine(cap, tok_rows)

    def drain(k):
        for make in (ag1x, ag1y, ag2x, ag2y, rs1x, rs1y, rs2x, rs2y):
            make(k).wait_send()

    each(nch, drain)
    each(nch, lambda k: give(k).wait_send(), give_from)
    each(hand_to, lambda k: hand_light(k).wait_send(), hand_from)


def moe_call(heavy_core, light_rows, number, tokens, ids, gates, their_ids, w_gate, w_up, w_down):
    tok_rows, width = tokens.shape
    tensor, _, hidden = w_gate.shape
    chunk = tok_rows // 16
    bf16 = jnp.bfloat16
    vmem = pl.BlockSpec(memory_space=pltpu.VMEM)
    hbm = pl.BlockSpec(memory_space=pl.ANY)
    return pl.pallas_call(
        functools.partial(moe_kernel, heavy_core, light_rows, chunk, 2),
        out_shape=jax.ShapeDtypeStruct((tok_rows, width), bf16),
        in_specs=[vmem, vmem, vmem, vmem, hbm, hbm, hbm],
        out_specs=vmem,
        scratch_shapes=[
            pltpu.VMEM((tensor, tok_rows, width), bf16),
            pltpu.VMEM((2, tensor, width, hidden), bf16),
            pltpu.VMEM((tensor, hidden, width), bf16),
            pltpu.VMEM((tok_rows, width), bf16),
            pltpu.VMEM((tok_rows, width), bf16),
            pltpu.VMEM((2, 4 * chunk, hidden), jnp.float32),
            pltpu.VMEM((3, tok_rows, width), bf16),
            pltpu.VMEM((tok_rows, width), bf16),
            pltpu.VMEM((tok_rows, width), bf16),
            pltpu.VMEM((tok_rows, width), bf16),
            pltpu.VMEM((tok_rows, width), jnp.float32),
            pltpu.VMEM((2, tok_rows, width), bf16),
            pltpu.VMEM((tok_rows, tok_rows // 2), bf16),
            pltpu.VMEM((tok_rows, tok_rows), bf16),
            pltpu.SemaphoreType.DMA((10, 16)),
            pltpu.SemaphoreType.DMA((10, 16)),
            pltpu.SemaphoreType.DMA((3, 4)),
        ],
        compiler_params=pltpu.CompilerParams(
            collective_id=number, has_side_effects=True, vmem_limit_bytes=60 * 1024 * 1024
        ),
        cost_estimate=pl.CostEstimate(
            flops=6 * tok_rows * tensor * width * hidden,
            bytes_accessed=6 * tensor * width * hidden,
            transcendentals=0,
        ),
    )(tokens, ids, gates, their_ids, w_gate, w_up, w_down)


def fused(tokens, route_ids, route_gates, w_gate, w_up, w_down):
    tok_rows, width = tokens.shape
    tensor = lax.axis_size("tensor")
    hidden = w_gate.shape[2]
    ids, gates = route_ids.T, route_gates.T
    their_ids = lax.ppermute(ids, "expert", [(0, 1), (1, 0)])
    shift = (2 * tok_rows).bit_length()
    unit = 1 << shift

    def tally(names):
        return jnp.where(names == 0, 1, 0) + jnp.where(names == 1, unit, 0)

    both = jnp.sum(tally(ids) + tally(their_ids))
    total_0, total_1 = both & (unit - 1), both >> shift
    sizes = (tok_rows // 2, tok_rows * 9 // 16, tok_rows * 5 // 8)
    plans = [(core, size) for size in sizes + (tok_rows,) for core in range(2)]
    least = jnp.minimum(total_0, total_1)
    level = sum((least > s).astype(jnp.int32) for s in sizes)
    heavy = (total_1 > total_0).astype(jnp.int32)
    index = 2 * level + heavy
    branches = [functools.partial(moe_call, *plan, n) for n, plan in enumerate(plans)]
    return lax.switch(
        index,
        branches,
        tokens,
        ids,
        gates,
        their_ids,
        w_gate.reshape(tensor, width, hidden),
        w_up.reshape(tensor, width, hidden),
        w_down.reshape(hidden, tensor * width),
    )


def general(tokens, route_ids, route_gates, w_gate, w_up, w_down):
    tok_rows, width_dev = tokens.shape
    picks = route_ids.shape[1]
    n_source = lax.axis_size("expert")
    local_count = w_gate.shape[0]
    n_flight = n_source * local_count
    capacity = tok_rows // 2
    flat_ids = route_ids.reshape(-1)
    onehot = (flat_ids[:, None] == jnp.arange(n_flight, dtype=jnp.int32)[None, :]).astype(jnp.int32)
    earlier = jnp.cumsum(onehot, axis=0) - onehot
    position = jnp.sum(earlier * onehot, axis=1)
    in_window = flat_ids < n_flight
    slots = jnp.where(in_window, flat_ids * capacity + position, n_flight * capacity)
    repeated = jnp.repeat(tokens, picks, axis=0)
    buffer = (
        jnp.zeros((n_flight * capacity, width_dev), jnp.bfloat16)
        .at[slots]
        .set(repeated, mode="drop")
    )
    buffer = buffer.reshape(n_flight, capacity, width_dev)
    received = lax.all_to_all(buffer, "expert", split_axis=0, concat_axis=0, tiled=True)
    piece = lax.all_gather(received, "tensor", axis=2, tiled=True)
    columns = piece.shape[2]
    grouped = piece.reshape(n_source, local_count, capacity, columns)
    gate = jnp.einsum("secd,edf->secf", grouped, w_gate, preferred_element_type=jnp.float32)
    upper = jnp.einsum("secd,edf->secf", grouped, w_up, preferred_element_type=jnp.float32)
    gated = (jax.nn.silu(gate) * upper).astype(jnp.bfloat16)
    partial_out = jnp.einsum("secf,efd->secd", gated, w_down, preferred_element_type=jnp.float32)
    partial_out = partial_out.reshape(n_flight, capacity, partial_out.shape[3])
    summed = lax.psum_scatter(partial_out, "tensor", scatter_dimension=2, tiled=True)
    expert_out = summed.astype(jnp.bfloat16)
    back = lax.all_to_all(expert_out, "expert", split_axis=0, concat_axis=0, tiled=True)
    flat_back = back.reshape(n_flight * capacity, width_dev)
    picked = jnp.take(flat_back, slots, axis=0, mode="fill", fill_value=0).astype(jnp.float32)
    picked = picked.reshape(tok_rows, picks, width_dev)
    mixed = jnp.sum(picked * route_gates[:, :, None], axis=1)
    return mixed.astype(jnp.bfloat16)


def solution(mesh):
    placed = (
        P(("dp", "expert"), "tensor"),
        P(("dp", "expert"), None),
        P(("dp", "expert"), None),
        P("expert", None, "tensor"),
        P("expert", None, "tensor"),
        P("expert", "tensor", None),
    )
    square = mesh.shape["tensor"] == 4 and mesh.shape["expert"] == 2
    return jax.shard_map(
        fused if square else general,
        mesh=mesh,
        in_specs=placed,
        out_specs=P(("dp", "expert"), "tensor"),
        check_vma=False,
    )
```

```python
import functools

import jax
import jax.numpy as jnp
from jax import lax
from jax.experimental import pallas as pl
from jax.experimental.pallas import tpu as pltpu
from jax.sharding import PartitionSpec as P

MESH = pl.DeviceIdType.MESH
AG1X, AG1Y, AG2X, AG2Y, RS1X, RS1Y, RS2X, RS2Y, RET, HAND = range(10)


def moe_kernel(
    heavy_core,
    light_rows,
    chunk,
    ahead,
    tok_ref,
    ids_ref,
    gat_ref,
    their_ids_ref,
    wg_hbm,
    wu_hbm,
    wd_hbm,
    out_ref,
    xg,
    wgu,
    wd,
    dsp,
    mrg,
    acc,
    snd,
    got_d,
    got_x,
    got_y,
    own,
    back,
    pt_own,
    pt_oth,
    send_sem,
    recv_sem,
    wsem,
):
    tok_rows, width = tok_ref.shape
    hidden = wgu.shape[3]
    cap = tok_rows // 2
    hc = chunk // 2
    tile = width // 3
    e = lax.axis_index("expert")
    t = lax.axis_index("tensor")
    tx = (t // 2) * 2 + (1 - t % 2)
    ty = (1 - t // 2) * 2 + t % 2
    td = 3 - t
    to_x, to_y, to_p = {"tensor": tx}, {"tensor": ty}, {"expert": 1 - e}
    most, least = tok_rows // chunk, light_rows // chunk
    heavy = (e - heavy_core) == 0
    light = jnp.logical_not(heavy)
    away = (e - heavy_core) * (e - heavy_core)
    nch = most - away * (most - least)
    per = 2
    block = per * chunk
    steps = (nch + per - 1) // per
    half = cap // chunk
    hand_from, hand_to = away * half, least + away * (most - least)
    got_from, got_to = half - away * half, most - away * (most - least)
    give_from = half - away * half
    take_from = away * half
    oth_nch = least + away * (most - least)

    barrier = pltpu.get_barrier_semaphore()
    for device in (to_p, to_x, to_y):
        pl.semaphore_signal(barrier, inc=1, device_id=device, device_id_type=MESH)

    def weight_copies():
        copies = []
        for s in range(4):
            copies.append(pltpu.make_async_copy(wg_hbm.at[s], wgu.at[0, s], wsem.at[0, s]))
            copies.append(pltpu.make_async_copy(wu_hbm.at[s], wgu.at[1, s], wsem.at[1, s]))
            there = wd_hbm.at[:, pl.ds(s * width, width)]
            copies.append(pltpu.make_async_copy(there, wd.at[s], wsem.at[2, s]))
        return copies

    for c in weight_copies():
        c.start()

    def rows(k):
        return pl.ds(pl.multiple_of(k * chunk, chunk), chunk)

    def first(k):
        return pl.ds(pl.multiple_of(k * chunk, hc), hc)

    def second(k):
        return pl.ds(pl.multiple_of(k * chunk + hc, hc), hc)

    def remote(kind, k, src, dst, device):
        return pltpu.make_async_remote_copy(
            src_ref=src,
            dst_ref=dst,
            send_sem=send_sem.at[kind, k],
            recv_sem=recv_sem.at[kind, k],
            device_id=device,
            device_id_type=MESH,
        )

    def ag1x(k):
        return remote(AG1X, k, xg.at[t, rows(k)], xg.at[t, rows(k)], to_x)

    def ag1y(k):
        return remote(AG1Y, k, xg.at[t, rows(k)], xg.at[t, rows(k)], to_y)

    def ag2x(k):
        return remote(AG2X, k, xg.at[ty, second(k)], xg.at[ty, second(k)], to_x)

    def ag2y(k):
        return remote(AG2Y, k, xg.at[tx, first(k)], xg.at[tx, first(k)], to_y)

    def rs1x(k):
        return remote(RS1X, k, snd.at[0, first(k)], got_d.at[first(k)], to_x)

    def rs1y(k):
        return remote(RS1Y, k, snd.at[0, second(k)], got_d.at[second(k)], to_y)

    def rs2x(k):
        return remote(RS2X, k, snd.at[1, rows(k)], got_x.at[rows(k)], to_x)

    def rs2y(k):
        return remote(RS2Y, k, snd.at[2, rows(k)], got_y.at[rows(k)], to_y)

    def give(k):
        return remote(RET, k, back.at[0, rows(k)], back.at[1, rows(k)], to_p)

    def hand_light(k):
        return remote(HAND, k, dsp.at[rows(k)], mrg.at[rows(k)], to_p)

    def hand_heavy(k):
        return remote(HAND, k, dsp.at[rows(k)], xg.at[t, rows(k)], to_p)

    def each(count, act, start=0):
        def go(k, carry):
            act(k)
            return carry

        lax.fori_loop(start, count, go, 0)

    before = (
        lax.broadcasted_iota(jnp.int32, (tok_rows, tok_rows), 0)
        < lax.broadcasted_iota(jnp.int32, (tok_rows, tok_rows), 1)
    )
    before = jnp.where(before, 1.0, 0.0).astype(jnp.bfloat16)

    def onehot(expert, count, offset):
        named = (ids_ref[0:1, :] == expert) | (ids_ref[1:2, :] == expert)
        named = jnp.where(named, 1.0, 0.0)
        wide = jnp.broadcast_to(named, (16, tok_rows)).astype(jnp.bfloat16)
        pos = jnp.dot(wide, before, preferred_element_type=jnp.float32)[0:1, :]
        pos = jnp.where(named > 0.5, pos, -2.0 * tok_rows).astype(jnp.int32) + offset
        slot = lax.broadcasted_iota(jnp.int32, (count, tok_rows), 0)
        return jnp.where(slot == pos, 1.0, 0.0)

    def gate_column(expert):
        row = jnp.where(ids_ref[0:1, :] == expert, gat_ref[0:1, :], 0.0)
        row += jnp.where(ids_ref[1:2, :] == expert, gat_ref[1:2, :], 0.0)
        return jnp.broadcast_to(row, (8, tok_rows)).T[:, 0:1]

    def columns(c):
        return pl.ds(pl.multiple_of(c * tile, 128), tile)

    def pieces(k, act):
        def go(j, carry):
            p = per * k + j
            pl.when((p >= 0) & (p < nch))(functools.partial(act, p))
            return carry

        lax.fori_loop(0, per, go, 0)

    def block_rows(k):
        return pl.ds(pl.multiple_of(k * block, block), block)

    def send_piece(p):
        ag1x(p).start()
        ag1y(p).start()

    def forward_piece(p):
        ag1x(p).wait_recv()
        ag2y(p).start()
        ag1y(p).wait_recv()
        ag2x(p).start()

    def gathered_piece(p):
        ag2x(p).wait_recv()
        ag2y(p).wait_recv()

    def reduce_piece(p):
        rs1x(p).start()
        rs1y(p).start()

    def add_piece(p):
        rs1x(p).wait_recv()
        snd[2, first(p), :] = (
            snd[2, first(p), :].astype(jnp.float32) + got_d[first(p), :].astype(jnp.float32)
        ).astype(jnp.bfloat16)
        rs2y(p).start()
        rs1y(p).wait_recv()
        snd[1, second(p), :] = (
            snd[1, second(p), :].astype(jnp.float32) + got_d[second(p), :].astype(jnp.float32)
        ).astype(jnp.bfloat16)
        rs2x(p).start()

    def finish_piece(p):
        rs2x(p).wait_recv()
        rs2y(p).wait_recv()
        back[0, rows(p), :] = (
            own[rows(p), :]
            + got_x[rows(p), :].astype(jnp.float32)
            + got_y[rows(p), :].astype(jnp.float32)
        ).astype(jnp.bfloat16)

        @pl.when(p >= give_from)
        def _():
            give(p).start()

    def ready(k):
        pieces(k, send_piece)

    pick_own = onehot(e, cap, 0)
    pick_own_b = pick_own.astype(jnp.bfloat16)

    @functools.partial(each, 3)
    def _(c):
        part = jnp.dot(pick_own_b, tok_ref[:, columns(c)], preferred_element_type=jnp.float32)
        xg[t, 0:cap, columns(c)] = part.astype(jnp.bfloat16)

    pl.semaphore_wait(barrier, 3)

    @pl.when(heavy)
    def _():
        each(ahead, ready)

    theirs_first = jnp.where(their_ids_ref[...] == 1 - e, 1.0, 0.0)
    offset = jnp.sum(jnp.sum(theirs_first, axis=1, keepdims=True), axis=0, keepdims=True)
    pick_oth = onehot(1 - e, tok_rows, offset.astype(jnp.int32))
    pick_oth_b = pick_oth.astype(jnp.bfloat16)

    def hand_over(lo, hi, hand):
        @functools.partial(each, 3)
        def _(c):
            part = jnp.dot(
                pick_oth_b[lo:hi], tok_ref[:, columns(c)], preferred_element_type=jnp.float32
            )
            dsp[lo:hi, columns(c)] = part.astype(jnp.bfloat16)

        each(hand_to, lambda k: hand(k).start(), hand_from)

    @pl.when(heavy)
    def _():
        hand_over(0, light_rows, hand_light)

    @pl.when(light)
    def _():
        hand_over(cap, tok_rows, hand_heavy)

    pt_own[...] = pick_own.T.astype(jnp.bfloat16)
    pt_oth[...] = pick_oth.T.astype(jnp.bfloat16)

    @pl.when(light)
    def _():
        each(got_to, lambda k: hand_light(k).wait_recv(), got_from)
        xg[t, 0:cap] = xg[t, 0:cap] + mrg[0:cap, :]
        if light_rows > cap:
            xg[t, cap:light_rows] = mrg[cap:light_rows, :]
        each(ahead, ready)

    def step(i, carry):
        @pl.when(heavy & (i + ahead == cap // block))
        def _():
            each(got_to, lambda k: hand_heavy(k).wait_recv(), got_from)

        ready(i + ahead)
        pieces(i, forward_piece)
        pieces(i - 2, add_piece)

        @pl.when(i == 1)
        def _():
            for c in weight_copies():
                c.wait()

        @pl.when((i >= 1) & (i - 1 < steps))
        def _():
            k = i - 1
            pieces(k, gathered_piece)
            acc[...] = jnp.zeros_like(acc)

            @functools.partial(each, 8)
            def _(n):
                s, j = n // 2, n % 2
                acc[j] += jnp.dot(
                    xg[s, block_rows(k), :], wgu[j, s], preferred_element_type=jnp.float32
                )

            gate = acc[0]
            gated = (gate / (1.0 + jnp.exp(-gate)) * acc[1]).astype(jnp.bfloat16)

            @functools.partial(each, 3)
            def _(r):
                towards = td + (tx - td) * ((r + 1) // 2) + (ty - tx) * (r // 2)
                part = jnp.dot(gated, wd[towards], preferred_element_type=jnp.float32)
                snd[r, block_rows(k), :] = part.astype(jnp.bfloat16)

                @pl.when(r == 0)
                def _():
                    pieces(k, reduce_piece)

            own[block_rows(k), :] = jnp.dot(gated, wd[t], preferred_element_type=jnp.float32)

        pieces(i - 3, finish_piece)
        return carry

    lax.fori_loop(0, steps + 3, step, 0)

    weight_own, weight_oth = gate_column(e), gate_column(1 - e)

    @functools.partial(each, 3)
    def _(c):
        mine = jnp.dot(
            pt_own[...], back[0, 0:cap, columns(c)], preferred_element_type=jnp.float32
        )
        own[:, columns(c)] = weight_own * mine

    each(oth_nch, lambda k: give(k).wait_recv(), take_from)

    def combine(lo, hi):
        @functools.partial(each, 3)
        def _(c):
            theirs = jnp.dot(
                pt_oth[:, lo:hi], back[1, lo:hi, columns(c)], preferred_element_type=jnp.float32
            )
            out_ref[:, columns(c)] = (own[:, columns(c)] + weight_oth * theirs).astype(
                jnp.bfloat16
            )

    @pl.when(heavy)
    def _():
        combine(0, light_rows)

    @pl.when(light)
    def _():
        combine(cap, tok_rows)

    def drain(k):
        for make in (ag1x, ag1y, ag2x, ag2y, rs1x, rs1y, rs2x, rs2y):
            make(k).wait_send()

    each(nch, drain)
    each(nch, lambda k: give(k).wait_send(), give_from)
    each(hand_to, lambda k: hand_light(k).wait_send(), hand_from)


def moe_call(heavy_core, light_rows, number, tokens, ids, gates, their_ids, w_gate, w_up, w_down):
    tok_rows, width = tokens.shape
    tensor, _, hidden = w_gate.shape
    chunk = tok_rows // 8
    bf16 = jnp.bfloat16
    vmem = pl.BlockSpec(memory_space=pltpu.VMEM)
    hbm = pl.BlockSpec(memory_space=pl.ANY)
    return pl.pallas_call(
        functools.partial(moe_kernel, heavy_core, light_rows, chunk, 2),
        out_shape=jax.ShapeDtypeStruct((tok_rows, width), bf16),
        in_specs=[vmem, vmem, vmem, vmem, hbm, hbm, hbm],
        out_specs=vmem,
        scratch_shapes=[
            pltpu.VMEM((tensor, tok_rows, width), bf16),
            pltpu.VMEM((2, tensor, width, hidden), bf16),
            pltpu.VMEM((tensor, hidden, width), bf16),
            pltpu.VMEM((tok_rows, width), bf16),
            pltpu.VMEM((tok_rows, width), bf16),
            pltpu.VMEM((2, 2 * chunk, hidden), jnp.float32),
            pltpu.VMEM((3, tok_rows, width), bf16),
            pltpu.VMEM((tok_rows, width), bf16),
            pltpu.VMEM((tok_rows, width), bf16),
            pltpu.VMEM((tok_rows, width), bf16),
            pltpu.VMEM((tok_rows, width), jnp.float32),
            pltpu.VMEM((2, tok_rows, width), bf16),
            pltpu.VMEM((tok_rows, tok_rows // 2), bf16),
            pltpu.VMEM((tok_rows, tok_rows), bf16),
            pltpu.SemaphoreType.DMA((10, 8)),
            pltpu.SemaphoreType.DMA((10, 8)),
            pltpu.SemaphoreType.DMA((3, 4)),
        ],
        compiler_params=pltpu.CompilerParams(
            collective_id=number, has_side_effects=True, vmem_limit_bytes=60 * 1024 * 1024
        ),
        cost_estimate=pl.CostEstimate(
            flops=6 * tok_rows * tensor * width * hidden,
            bytes_accessed=6 * tensor * width * hidden,
            transcendentals=0,
        ),
    )(tokens, ids, gates, their_ids, w_gate, w_up, w_down)


def fused(tokens, route_ids, route_gates, w_gate, w_up, w_down):
    tok_rows, width = tokens.shape
    tensor = lax.axis_size("tensor")
    hidden = w_gate.shape[2]
    ids, gates = route_ids.T, route_gates.T
    their_ids = lax.ppermute(ids, "expert", [(0, 1), (1, 0)])
    shift = (2 * tok_rows).bit_length()
    unit = 1 << shift

    def tally(names):
        return jnp.where(names == 0, 1, 0) + jnp.where(names == 1, unit, 0)

    both = jnp.sum(tally(ids) + tally(their_ids))
    total_0, total_1 = both & (unit - 1), both >> shift
    sizes = (tok_rows // 2, tok_rows * 5 // 8, tok_rows * 3 // 4)
    plans = [(core, size) for size in sizes + (tok_rows,) for core in range(2)]
    least = jnp.minimum(total_0, total_1)
    level = sum((least > s).astype(jnp.int32) for s in sizes)
    heavy = (total_1 > total_0).astype(jnp.int32)
    index = 2 * level + heavy
    branches = [functools.partial(moe_call, *plan, n) for n, plan in enumerate(plans)]
    return lax.switch(
        index,
        branches,
        tokens,
        ids,
        gates,
        their_ids,
        w_gate.reshape(tensor, width, hidden),
        w_up.reshape(tensor, width, hidden),
        w_down.reshape(hidden, tensor * width),
    )


def general(tokens, route_ids, route_gates, w_gate, w_up, w_down):
    tok_rows, width_dev = tokens.shape
    picks = route_ids.shape[1]
    n_source = lax.axis_size("expert")
    local_count = w_gate.shape[0]
    n_flight = n_source * local_count
    capacity = tok_rows // 2
    flat_ids = route_ids.reshape(-1)
    onehot = (flat_ids[:, None] == jnp.arange(n_flight, dtype=jnp.int32)[None, :]).astype(jnp.int32)
    earlier = jnp.cumsum(onehot, axis=0) - onehot
    position = jnp.sum(earlier * onehot, axis=1)
    in_window = flat_ids < n_flight
    slots = jnp.where(in_window, flat_ids * capacity + position, n_flight * capacity)
    repeated = jnp.repeat(tokens, picks, axis=0)
    buffer = (
        jnp.zeros((n_flight * capacity, width_dev), jnp.bfloat16)
        .at[slots]
        .set(repeated, mode="drop")
    )
    buffer = buffer.reshape(n_flight, capacity, width_dev)
    received = lax.all_to_all(buffer, "expert", split_axis=0, concat_axis=0, tiled=True)
    piece = lax.all_gather(received, "tensor", axis=2, tiled=True)
    columns = piece.shape[2]
    grouped = piece.reshape(n_source, local_count, capacity, columns)
    gate = jnp.einsum("secd,edf->secf", grouped, w_gate, preferred_element_type=jnp.float32)
    upper = jnp.einsum("secd,edf->secf", grouped, w_up, preferred_element_type=jnp.float32)
    gated = (jax.nn.silu(gate) * upper).astype(jnp.bfloat16)
    partial_out = jnp.einsum("secf,efd->secd", gated, w_down, preferred_element_type=jnp.float32)
    partial_out = partial_out.reshape(n_flight, capacity, partial_out.shape[3])
    summed = lax.psum_scatter(partial_out, "tensor", scatter_dimension=2, tiled=True)
    expert_out = summed.astype(jnp.bfloat16)
    back = lax.all_to_all(expert_out, "expert", split_axis=0, concat_axis=0, tiled=True)
    flat_back = back.reshape(n_flight * capacity, width_dev)
    picked = jnp.take(flat_back, slots, axis=0, mode="fill", fill_value=0).astype(jnp.float32)
    picked = picked.reshape(tok_rows, picks, width_dev)
    mixed = jnp.sum(picked * route_gates[:, :, None], axis=1)
    return mixed.astype(jnp.bfloat16)


def solution(mesh):
    placed = (
        P(("dp", "expert"), "tensor"),
        P(("dp", "expert"), None),
        P(("dp", "expert"), None),
        P("expert", None, "tensor"),
        P("expert", None, "tensor"),
        P("expert", "tensor", None),
    )
    square = mesh.shape["tensor"] == 4 and mesh.shape["expert"] == 2
    return jax.shard_map(
        fused if square else general,
        mesh=mesh,
        in_specs=placed,
        out_specs=P(("dp", "expert"), "tensor"),
        check_vma=False,
    )
```

```python
import functools

import jax
import jax.numpy as jnp
from jax import lax
from jax.experimental import pallas as pl
from jax.experimental.pallas import tpu as pltpu
from jax.sharding import PartitionSpec as P

MESH = pl.DeviceIdType.MESH
AG1X, AG1Y, AG2X, AG2Y, RS1X, RS1Y, RS2X, RS2Y, RET, HAND = range(10)


def moe_kernel(
    heavy_core,
    light_rows,
    chunk,
    ahead,
    tok_ref,
    ids_ref,
    gat_ref,
    their_ids_ref,
    wg_hbm,
    wu_hbm,
    wd_hbm,
    out_ref,
    xg,
    wgu,
    wd,
    dsp,
    mrg,
    acc,
    snd,
    got_d,
    got_x,
    got_y,
    own,
    back,
    pt_own,
    pt_oth,
    send_sem,
    recv_sem,
    wsem,
):
    tok_rows, width = tok_ref.shape
    hidden = wgu.shape[3]
    cap = tok_rows // 2
    hc = chunk // 2
    tile = width // 3
    e = lax.axis_index("expert")
    t = lax.axis_index("tensor")
    tx = (t // 2) * 2 + (1 - t % 2)
    ty = (1 - t // 2) * 2 + t % 2
    td = 3 - t
    to_x, to_y, to_p = {"tensor": tx}, {"tensor": ty}, {"expert": 1 - e}
    most, least = tok_rows // chunk, light_rows // chunk
    heavy = (e - heavy_core) == 0
    away = (e - heavy_core) * (e - heavy_core)
    nch = most - away * (most - least)
    steps = (nch + 1) // 2
    block = 2 * chunk
    oth_nch = least + away * (most - least)

    barrier = pltpu.get_barrier_semaphore()
    for device in (to_p, to_x, to_y):
        pl.semaphore_signal(barrier, inc=1, device_id=device, device_id_type=MESH)

    def weight_copies():
        copies = []
        for s in range(4):
            copies.append(pltpu.make_async_copy(wg_hbm.at[s], wgu.at[0, s], wsem.at[0, s]))
            copies.append(pltpu.make_async_copy(wu_hbm.at[s], wgu.at[1, s], wsem.at[1, s]))
            there = wd_hbm.at[:, pl.ds(s * width, width)]
            copies.append(pltpu.make_async_copy(there, wd.at[s], wsem.at[2, s]))
        return copies

    for c in weight_copies():
        c.start()

    def rows(k):
        return pl.ds(pl.multiple_of(k * chunk, chunk), chunk)

    def first(k):
        return pl.ds(pl.multiple_of(k * chunk, hc), hc)

    def second(k):
        return pl.ds(pl.multiple_of(k * chunk + hc, hc), hc)

    def remote(kind, k, src, dst, device):
        return pltpu.make_async_remote_copy(
            src_ref=src,
            dst_ref=dst,
            send_sem=send_sem.at[kind, k],
            recv_sem=recv_sem.at[kind, k],
            device_id=device,
            device_id_type=MESH,
        )

    def ag1x(k):
        return remote(AG1X, k, xg.at[t, rows(k)], xg.at[t, rows(k)], to_x)

    def ag1y(k):
        return remote(AG1Y, k, xg.at[t, rows(k)], xg.at[t, rows(k)], to_y)

    def ag2x(k):
        return remote(AG2X, k, xg.at[ty, second(k)], xg.at[ty, second(k)], to_x)

    def ag2y(k):
        return remote(AG2Y, k, xg.at[tx, first(k)], xg.at[tx, first(k)], to_y)

    def rs1x(k):
        return remote(RS1X, k, snd.at[0, first(k)], got_d.at[first(k)], to_x)

    def rs1y(k):
        return remote(RS1Y, k, snd.at[0, second(k)], got_d.at[second(k)], to_y)

    def rs2x(k):
        return remote(RS2X, k, snd.at[1, rows(k)], got_x.at[rows(k)], to_x)

    def rs2y(k):
        return remote(RS2Y, k, snd.at[2, rows(k)], got_y.at[rows(k)], to_y)

    def give(k):
        return remote(RET, k, back.at[0, rows(k)], back.at[1, rows(k)], to_p)

    def hand(k):
        return remote(HAND, k, dsp.at[rows(k)], mrg.at[rows(k)], to_p)

    def each(count, act, start=0):
        def go(k, carry):
            act(k)
            return carry

        lax.fori_loop(start, count, go, 0)

    before = (
        lax.broadcasted_iota(jnp.int32, (tok_rows, tok_rows), 0)
        < lax.broadcasted_iota(jnp.int32, (tok_rows, tok_rows), 1)
    )
    before = jnp.where(before, 1.0, 0.0).astype(jnp.bfloat16)

    def onehot(expert, count, offset):
        named = (ids_ref[0:1, :] == expert) | (ids_ref[1:2, :] == expert)
        named = jnp.where(named, 1.0, 0.0)
        wide = jnp.broadcast_to(named, (16, tok_rows)).astype(jnp.bfloat16)
        pos = jnp.dot(wide, before, preferred_element_type=jnp.float32)[0:1, :]
        pos = jnp.where(named > 0.5, pos, -2.0 * tok_rows).astype(jnp.int32) + offset
        slot = lax.broadcasted_iota(jnp.int32, (count, tok_rows), 0)
        return jnp.where(slot == pos, 1.0, 0.0)

    def gate_column(expert):
        row = jnp.where(ids_ref[0:1, :] == expert, gat_ref[0:1, :], 0.0)
        row += jnp.where(ids_ref[1:2, :] == expert, gat_ref[1:2, :], 0.0)
        return jnp.broadcast_to(row, (8, tok_rows)).T[:, 0:1]

    def columns(c):
        return pl.ds(pl.multiple_of(c * tile, 128), tile)

    def pieces(k, act):
        for p in (2 * k, 2 * k + 1):
            pl.when((p >= 0) & (p < nch))(functools.partial(act, p))

    def block_rows(k):
        return pl.ds(pl.multiple_of(k * block, block), block)

    def send_piece(p):
        ag1x(p).start()
        ag1y(p).start()

    def forward_piece(p):
        ag1x(p).wait_recv()
        ag2y(p).start()
        ag1y(p).wait_recv()
        ag2x(p).start()

    def gathered_piece(p):
        ag2x(p).wait_recv()
        ag2y(p).wait_recv()

    def reduce_piece(p):
        rs1x(p).start()
        rs1y(p).start()

    def add_piece(p):
        rs1x(p).wait_recv()
        snd[2, first(p), :] = (
            snd[2, first(p), :].astype(jnp.float32) + got_d[first(p), :].astype(jnp.float32)
        ).astype(jnp.bfloat16)
        rs2y(p).start()
        rs1y(p).wait_recv()
        snd[1, second(p), :] = (
            snd[1, second(p), :].astype(jnp.float32) + got_d[second(p), :].astype(jnp.float32)
        ).astype(jnp.bfloat16)
        rs2x(p).start()

    def finish_piece(p):
        rs2x(p).wait_recv()
        rs2y(p).wait_recv()
        back[0, rows(p), :] = (
            own[rows(p), :]
            + got_x[rows(p), :].astype(jnp.float32)
            + got_y[rows(p), :].astype(jnp.float32)
        ).astype(jnp.bfloat16)
        give(p).start()

    def ready(k):
        pieces(k, send_piece)

    def merge(lo, hi):
        each(nch, lambda k: hand(k).wait_recv())
        xg[t, lo:hi] = xg[t, lo:hi] + mrg[lo:hi, :]

    pick_own = onehot(e, cap, 0)
    pick_own_b = pick_own.astype(jnp.bfloat16)

    @functools.partial(each, 3)
    def _(c):
        part = jnp.dot(pick_own_b, tok_ref[:, columns(c)], preferred_element_type=jnp.float32)
        xg[t, 0:cap, columns(c)] = part.astype(jnp.bfloat16)

    pl.semaphore_wait(barrier, 3)

    @pl.when(heavy)
    def _():
        each(ahead, ready)

    xg[t, cap:tok_rows] = jnp.zeros((tok_rows - cap, width), jnp.bfloat16)
    theirs_first = jnp.where(their_ids_ref[...] == 1 - e, 1.0, 0.0)
    offset = jnp.sum(jnp.sum(theirs_first, axis=1, keepdims=True), axis=0, keepdims=True)
    pick_oth = onehot(1 - e, tok_rows, offset.astype(jnp.int32))
    pick_oth_b = pick_oth.astype(jnp.bfloat16)

    @functools.partial(each, 3)
    def _(c):
        part = jnp.dot(pick_oth_b, tok_ref[:, columns(c)], preferred_element_type=jnp.float32)
        dsp[:, columns(c)] = part.astype(jnp.bfloat16)

    each(oth_nch, lambda k: hand(k).start())
    pt_own[...] = pick_own.T.astype(jnp.bfloat16)
    pt_oth[...] = pick_oth.T.astype(jnp.bfloat16)

    @pl.when(heavy)
    def _():
        if light_rows < tok_rows:
            gap = tok_rows - light_rows
            back[1, light_rows:tok_rows] = jnp.zeros((gap, width), jnp.bfloat16)

    @pl.when(jnp.logical_not(heavy))
    def _():
        merge(0, light_rows)
        each(ahead, ready)

    def step(i, carry):
        @pl.when(heavy & (i + ahead == cap // block))
        def _():
            merge(cap, tok_rows)

        ready(i + ahead)
        pieces(i, forward_piece)

        @pl.when(i == 1)
        def _():
            for c in weight_copies():
                c.wait()

        @pl.when((i >= 1) & (i - 1 < steps))
        def _():
            k = i - 1
            pieces(k, gathered_piece)
            acc[...] = jnp.zeros_like(acc)

            @functools.partial(each, 8)
            def _(n):
                s, j = n // 2, n % 2
                acc[j] += jnp.dot(
                    xg[s, block_rows(k), :], wgu[j, s], preferred_element_type=jnp.float32
                )

            gate = acc[0]
            gated = (gate / (1.0 + jnp.exp(-gate)) * acc[1]).astype(jnp.bfloat16)

            @functools.partial(each, 3)
            def _(r):
                towards = td + (tx - td) * ((r + 1) // 2) + (ty - tx) * (r // 2)
                part = jnp.dot(gated, wd[towards], preferred_element_type=jnp.float32)
                snd[r, block_rows(k), :] = part.astype(jnp.bfloat16)

                @pl.when(r == 0)
                def _():
                    pieces(k, reduce_piece)

            own[block_rows(k), :] = jnp.dot(gated, wd[t], preferred_element_type=jnp.float32)

        pieces(i - 2, add_piece)
        pieces(i - 3, finish_piece)
        return carry

    lax.fori_loop(0, steps + 3, step, 0)

    each(oth_nch, lambda k: give(k).wait_recv())
    weight_own, weight_oth = gate_column(e), gate_column(1 - e)

    @functools.partial(each, 3)
    def _(c):
        mine = jnp.dot(
            pt_own[...], back[0, 0:cap, columns(c)], preferred_element_type=jnp.float32
        )
        theirs = jnp.dot(pt_oth[...], back[1, :, columns(c)], preferred_element_type=jnp.float32)
        out_ref[:, columns(c)] = (weight_own * mine + weight_oth * theirs).astype(jnp.bfloat16)

    def drain(k):
        for make in (ag1x, ag1y, ag2x, ag2y, rs1x, rs1y, rs2x, rs2y, give):
            make(k).wait_send()

    each(nch, drain)
    each(oth_nch, lambda k: hand(k).wait_send())


def moe_call(heavy_core, light_rows, number, tokens, ids, gates, their_ids, w_gate, w_up, w_down):
    tok_rows, width = tokens.shape
    tensor, _, hidden = w_gate.shape
    chunk = tok_rows // 8
    bf16 = jnp.bfloat16
    vmem = pl.BlockSpec(memory_space=pltpu.VMEM)
    hbm = pl.BlockSpec(memory_space=pl.ANY)
    return pl.pallas_call(
        functools.partial(moe_kernel, heavy_core, light_rows, chunk, 2),
        out_shape=jax.ShapeDtypeStruct((tok_rows, width), bf16),
        in_specs=[vmem, vmem, vmem, vmem, hbm, hbm, hbm],
        out_specs=vmem,
        scratch_shapes=[
            pltpu.VMEM((tensor, tok_rows, width), bf16),
            pltpu.VMEM((2, tensor, width, hidden), bf16),
            pltpu.VMEM((tensor, hidden, width), bf16),
            pltpu.VMEM((tok_rows, width), bf16),
            pltpu.VMEM((tok_rows, width), bf16),
            pltpu.VMEM((2, 2 * chunk, hidden), jnp.float32),
            pltpu.VMEM((3, tok_rows, width), bf16),
            pltpu.VMEM((tok_rows, width), bf16),
            pltpu.VMEM((tok_rows, width), bf16),
            pltpu.VMEM((tok_rows, width), bf16),
            pltpu.VMEM((tok_rows, width), jnp.float32),
            pltpu.VMEM((2, tok_rows, width), bf16),
            pltpu.VMEM((tok_rows, tok_rows // 2), bf16),
            pltpu.VMEM((tok_rows, tok_rows), bf16),
            pltpu.SemaphoreType.DMA((10, 8)),
            pltpu.SemaphoreType.DMA((10, 8)),
            pltpu.SemaphoreType.DMA((3, 4)),
        ],
        compiler_params=pltpu.CompilerParams(
            collective_id=number, has_side_effects=True, vmem_limit_bytes=60 * 1024 * 1024
        ),
        cost_estimate=pl.CostEstimate(
            flops=6 * tok_rows * tensor * width * hidden,
            bytes_accessed=6 * tensor * width * hidden,
            transcendentals=0,
        ),
    )(tokens, ids, gates, their_ids, w_gate, w_up, w_down)


def fused(tokens, route_ids, route_gates, w_gate, w_up, w_down):
    tok_rows, width = tokens.shape
    tensor = lax.axis_size("tensor")
    hidden = w_gate.shape[2]
    ids, gates = route_ids.T, route_gates.T
    their_ids = lax.ppermute(ids, "expert", [(0, 1), (1, 0)])
    shift = (2 * tok_rows).bit_length()
    unit = 1 << shift

    def tally(names):
        return jnp.where(names == 0, 1, 0) + jnp.where(names == 1, unit, 0)

    both = jnp.sum(tally(ids) + tally(their_ids))
    total_0, total_1 = both & (unit - 1), both >> shift
    sizes = (tok_rows // 2, tok_rows * 5 // 8, tok_rows * 3 // 4)
    plans = [(core, size) for size in sizes + (tok_rows,) for core in range(2)]
    least = jnp.minimum(total_0, total_1)
    level = sum((least > s).astype(jnp.int32) for s in sizes)
    heavy = (total_1 > total_0).astype(jnp.int32)
    index = 2 * level + heavy
    branches = [functools.partial(moe_call, *plan, n) for n, plan in enumerate(plans)]
    return lax.switch(
        index,
        branches,
        tokens,
        ids,
        gates,
        their_ids,
        w_gate.reshape(tensor, width, hidden),
        w_up.reshape(tensor, width, hidden),
        w_down.reshape(hidden, tensor * width),
    )


def general(tokens, route_ids, route_gates, w_gate, w_up, w_down):
    tok_rows, width_dev = tokens.shape
    picks = route_ids.shape[1]
    n_source = lax.axis_size("expert")
    local_count = w_gate.shape[0]
    n_flight = n_source * local_count
    capacity = tok_rows // 2
    flat_ids = route_ids.reshape(-1)
    onehot = (flat_ids[:, None] == jnp.arange(n_flight, dtype=jnp.int32)[None, :]).astype(jnp.int32)
    earlier = jnp.cumsum(onehot, axis=0) - onehot
    position = jnp.sum(earlier * onehot, axis=1)
    in_window = flat_ids < n_flight
    slots = jnp.where(in_window, flat_ids * capacity + position, n_flight * capacity)
    repeated = jnp.repeat(tokens, picks, axis=0)
    buffer = (
        jnp.zeros((n_flight * capacity, width_dev), jnp.bfloat16)
        .at[slots]
        .set(repeated, mode="drop")
    )
    buffer = buffer.reshape(n_flight, capacity, width_dev)
    received = lax.all_to_all(buffer, "expert", split_axis=0, concat_axis=0, tiled=True)
    piece = lax.all_gather(received, "tensor", axis=2, tiled=True)
    columns = piece.shape[2]
    grouped = piece.reshape(n_source, local_count, capacity, columns)
    gate = jnp.einsum("secd,edf->secf", grouped, w_gate, preferred_element_type=jnp.float32)
    upper = jnp.einsum("secd,edf->secf", grouped, w_up, preferred_element_type=jnp.float32)
    gated = (jax.nn.silu(gate) * upper).astype(jnp.bfloat16)
    partial_out = jnp.einsum("secf,efd->secd", gated, w_down, preferred_element_type=jnp.float32)
    partial_out = partial_out.reshape(n_flight, capacity, partial_out.shape[3])
    summed = lax.psum_scatter(partial_out, "tensor", scatter_dimension=2, tiled=True)
    expert_out = summed.astype(jnp.bfloat16)
    back = lax.all_to_all(expert_out, "expert", split_axis=0, concat_axis=0, tiled=True)
    flat_back = back.reshape(n_flight * capacity, width_dev)
    picked = jnp.take(flat_back, slots, axis=0, mode="fill", fill_value=0).astype(jnp.float32)
    picked = picked.reshape(tok_rows, picks, width_dev)
    mixed = jnp.sum(picked * route_gates[:, :, None], axis=1)
    return mixed.astype(jnp.bfloat16)


def solution(mesh):
    placed = (
        P(("dp", "expert"), "tensor"),
        P(("dp", "expert"), None),
        P(("dp", "expert"), None),
        P("expert", None, "tensor"),
        P("expert", None, "tensor"),
        P("expert", "tensor", None),
    )
    square = mesh.shape["tensor"] == 4 and mesh.shape["expert"] == 2
    return jax.shard_map(
        fused if square else general,
        mesh=mesh,
        in_specs=placed,
        out_specs=P(("dp", "expert"), "tensor"),
        check_vma=False,
    )
```
